32 devices in a mesh: pipe: 2 (over core), dp: 16 (over z, y, x).
Axes of the slice: x: 2, y: 2, z: 4, core: 2. Of those that a mesh axis runs over, the one named last changes fastest.
Arguments:
- page_inputs: bfloat16 [48, 20, 20, 512], P('dp', None, None, 'pipe'), may hold values from -6 to 6
- gain_one: bfloat16 [2, 512], P('pipe'), may hold values from 0.5 to 1.5
- bias_one: bfloat16 [2, 512], P('pipe'), may hold values from -3 to 3
- qkv_weight: bfloat16 [2, 512, 1536], P('pipe'), may hold values from -0.25 to 0.25
- query_bias: bfloat16 [2, 512], P('pipe'), may hold values from -3 to 3
- value_bias: bfloat16 [2, 512], P('pipe'), may hold values from -3 to 3
- bias_table: bfloat16 [2, 361, 16], P('pipe'), may hold values from -4 to 4
- proj_weight: bfloat16 [2, 512, 512], P('pipe'), may hold values from -0.75 to 0.75
- proj_bias: bfloat16 [2, 512], P('pipe'), may hold values from -3 to 3
- gain_two: bfloat16 [2, 512], P('pipe'), may hold values from 0.5 to 1.5
- bias_two: bfloat16 [2, 512], P('pipe'), may hold values from -3 to 3
- fc1_weight: bfloat16 [2, 512, 2048], P('pipe'), may hold values from -0.25 to 0.25
- fc1_bias: bfloat16 [2, 2048], P('pipe'), may hold values from -3 to 3
- fc2_weight: bfloat16 [2, 2048, 512], P('pipe'), may hold values from -0.125 to 0.125
- fc2_bias: bfloat16 [2, 512], P('pipe'), may hold values from -3 to 3
- merge_gain: bfloat16 [2048], replicated, may hold values from 0.5 to 1.5
- merge_bias: bfloat16 [2048], replicated, may hold values from -3 to 3
- merge_weight: bfloat16 [2048, 1024], P(None, 'pipe'), may hold values from -0.125 to 0.125
- cotangent: bfloat16 [48, 10, 10, 1024], P('dp', None, None, 'pipe'), may hold values from -6 to 6
Outputs:
- merged: bfloat16 [48, 10, 10, 1024], P('dp', None, None, 'pipe')
- grad_page_inputs: float32 [48, 20, 20, 512], P('dp', None, None, 'pipe')
- grad_gain_one: float32 [2, 512], P('pipe')
- grad_bias_one: float32 [2, 512], P('pipe')
- grad_qkv_weight: float32 [2, 512, 1536], P('pipe')
- grad_query_bias: float32 [2, 512], P('pipe')
- grad_value_bias: float32 [2, 512], P('pipe')
- grad_bias_table: float32 [2, 361, 16], P('pipe')
- grad_proj_weight: float32 [2, 512, 512], P('pipe')
- grad_proj_bias: float32 [2, 512], P('pipe')
- grad_gain_two: float32 [2, 512], P('pipe')
- grad_bias_two: float32 [2, 512], P('pipe')
- grad_fc1_weight: float32 [2, 512, 2048], P('pipe')
- grad_fc1_bias: float32 [2, 2048], P('pipe')
- grad_fc2_weight: float32 [2, 2048, 512], P('pipe')
- grad_fc2_bias: float32 [2, 512], P('pipe')
- grad_merge_gain: float32 [2048], replicated
- grad_merge_bias: float32 [2048], replicated
- grad_merge_weight: float32 [2048, 1024], P(None, 'pipe')
The draws below stay inside these ranges and needn't reach their ends.
All inputs are finite; a program needn't handle non-finite values.
Results may differ from the reference program's by a relative error of at most 0.018.
Values may be sent and summed in bfloat16 or wider, within the bound.
A program may use at most 256 MiB of HBM per device.

```python
import jax
import jax.numpy as jnp
from jax import lax

D = 512
HEADS = 16
HEAD_DIM = 32
FF = 2048
WINDOW = 10
PAGE_H = 20
PAGE_W = 20
PAGES = 48
TABLE = 361
MERGE_IN = 2048
MERGE_OUT = 1024
N_PIPE = 2


def levels(key, dims, shards, least, largest):
    level = 1.0
    for dim, blocks in shards:
        steps = jax.random.uniform(jax.random.fold_in(jax.random.fold_in(key, 6), dim), (blocks,), jnp.float32, least / len(shards), largest / len(shards))
        level = level * jnp.repeat(jnp.exp(steps), dims[dim] // blocks).reshape((-1,) + (1,) * (len(dims) - 1 - dim))
    return level


def gaussian(key, dims, deviation, limit, shards=(), kind=jnp.bfloat16):
    factor_of = levels(key, dims, shards, -0.22, 0.18) if shards else 1.0
    result = jax.random.normal(key, dims, jnp.float32) * deviation * factor_of
    return jnp.minimum(jnp.maximum(result, -limit), limit).astype(kind)


def setup_inputs(seed: int = 0) -> dict:
    seeds = jax.random.split(jax.random.key(seed), 20)
    page_inputs = gaussian(seeds[0], (PAGES, PAGE_H, PAGE_W, D), 1.0, 6.0, ((0, 16), (3, 2)))
    gain_one = jnp.clip(1.0 + 0.1 * jax.random.normal(seeds[1], (2, D), jnp.float32), 0.5, 1.5).astype(jnp.bfloat16)
    bias_one = gaussian(seeds[2], (2, D), 0.5, 3.0, ((0, 2),))
    qkv_weight = gaussian(seeds[3], (2, D, 3 * D), D ** -0.5, 0.25, ((0, 2),))
    query_bias = gaussian(seeds[4], (2, D), 0.5, 3.0, ((0, 2),))
    value_bias = gaussian(seeds[5], (2, D), 0.5, 3.0, ((0, 2),))
    bias_table = gaussian(seeds[6], (2, TABLE, HEADS), 1.0, 4.0, ((0, 2),))
    proj_weight = gaussian(seeds[7], (2, D, D), (D // 8) ** -0.5, 0.75, ((0, 2),))
    proj_bias = gaussian(seeds[8], (2, D), 0.5, 3.0, ((0, 2),))
    gain_two = jnp.clip(1.0 + 0.1 * jax.random.normal(seeds[9], (2, D), jnp.float32), 0.5, 1.5).astype(jnp.bfloat16)
    bias_two = gaussian(seeds[10], (2, D), 0.5, 3.0, ((0, 2),))
    fc1_weight = gaussian(seeds[11], (2, D, FF), D ** -0.5, 0.25, ((0, 2),))
    fc1_bias = gaussian(seeds[12], (2, FF), 0.5, 3.0, ((0, 2),))
    fc2_weight = gaussian(seeds[13], (2, FF, D), FF ** -0.5, 0.125, ((0, 2),))
    fc2_bias = gaussian(seeds[14], (2, D), 0.5, 3.0, ((0, 2),))
    merge_gain = jnp.clip(1.0 + 0.1 * jax.random.normal(seeds[15], (MERGE_IN,), jnp.float32), 0.5, 1.5).astype(jnp.bfloat16)
    merge_bias = gaussian(seeds[16], (MERGE_IN,), 0.5, 3.0)
    merge_weight = gaussian(seeds[17], (MERGE_IN, MERGE_OUT), MERGE_IN ** -0.5, 0.125, ((1, 2),))
    cotangent = gaussian(seeds[18], (PAGES, PAGE_H // 2, PAGE_W // 2, MERGE_OUT), 1.0, 6.0, ((0, 16), (3, 2)))
    return dict(page_inputs=page_inputs, gain_one=gain_one, bias_one=bias_one, qkv_weight=qkv_weight, query_bias=query_bias, value_bias=value_bias, bias_table=bias_table, proj_weight=proj_weight, proj_bias=proj_bias, gain_two=gain_two, bias_two=bias_two, fc1_weight=fc1_weight, fc1_bias=fc1_bias, fc2_weight=fc2_weight, fc2_bias=fc2_bias, merge_gain=merge_gain, merge_bias=merge_bias, merge_weight=merge_weight, cotangent=cotangent)


@jax.custom_vjp
def low(v):
    return lax.optimization_barrier(v.astype(jnp.bfloat16)).astype(jnp.float32)

@jax.custom_vjp
def low_back(v):
    return v

def low_keep(v):
    return (low(v), None)

def low_pass(kept, grad):
    return (grad,)

def back_keep(v):
    return (v, None)

def back_low(kept, grad):
    return (low(grad),)
low.defvjp(low_keep, low_pass)
low_back.defvjp(back_keep, back_low)
norm_eps = 1e-05
highest = lax.Precision.HIGHEST

def layer_norm(values, scale_gain, shift_bias):
    average = lax.optimization_barrier(jnp.mean(values, axis=-1, keepdims=True))
    centred = values - average
    variance = lax.optimization_barrier(jnp.mean(centred * centred, axis=-1, keepdims=True))
    return centred * lax.rsqrt(variance + norm_eps) * scale_gain + shift_bias

def to_windows(spatial):
    page_count, grid_height, grid_width, channels = spatial.shape
    window_tiles = spatial.reshape(page_count, grid_height // WINDOW, WINDOW, grid_width // WINDOW, WINDOW, channels)
    return window_tiles.transpose(0, 1, 3, 2, 4, 5).reshape(-1, WINDOW * WINDOW, channels)

def from_windows(window_tiles, page_count):
    channels = window_tiles.shape[-1]
    spatial = window_tiles.reshape(page_count, PAGE_H // WINDOW, PAGE_W // WINDOW, WINDOW, WINDOW, channels)
    return spatial.transpose(0, 1, 3, 2, 4, 5).reshape(page_count, PAGE_H, PAGE_W, channels)

def relative_index():
    places = jnp.arange(WINDOW * WINDOW, dtype=jnp.int32)
    row_place = places // WINDOW
    col_place = places % WINDOW
    row_delta = row_place[:, None] - row_place[None, :] + WINDOW - 1
    col_delta = col_place[:, None] - col_place[None, :] + WINDOW - 1
    return (row_delta * (2 * WINDOW - 1) + col_delta).astype(jnp.int32)

def shift_mask():
    row_ids = jnp.arange(PAGE_H, dtype=jnp.int32)
    col_ids = jnp.arange(PAGE_W, dtype=jnp.int32)
    row_region = (row_ids >= PAGE_H - WINDOW).astype(jnp.int32) + (row_ids >= PAGE_H - WINDOW // 2).astype(jnp.int32)
    col_region = (col_ids >= PAGE_W - WINDOW).astype(jnp.int32) + (col_ids >= PAGE_W - WINDOW // 2).astype(jnp.int32)
    region = row_region[:, None] * 3 + col_region[None, :]
    region_tiles = to_windows(region[None, :, :, None])[:, :, 0]
    return jnp.where(region_tiles[:, :, None] != region_tiles[:, None, :], -100.0, 0.0).astype(jnp.float32)

def patch_merge(spatial):
    page_count, grid_height, grid_width, channels = spatial.shape
    quad_rows = spatial.reshape(page_count, grid_height // 2, 2, grid_width // 2, 2, channels)
    return quad_rows.transpose(0, 1, 3, 4, 2, 5).reshape(-1, 4 * channels)

def swin_block(inputs, weights, shifted):
    gain_one, bias_one, qkv_weight, query_bias, value_bias, bias_table, proj_weight, proj_bias, gain_two, bias_two, fc1_weight, fc1_bias, fc2_weight, fc2_bias = weights
    page_count = inputs.shape[0]
    if shifted:
        inputs = jnp.roll(inputs, (-(WINDOW // 2), -(WINDOW // 2)), axis=(1, 2))
    tokens = to_windows(inputs)
    window_count, window_area = (tokens.shape[0], tokens.shape[1])
    normed = low(layer_norm(tokens, gain_one, bias_one))
    projected = jnp.einsum('btd,de->bte', normed, qkv_weight, precision=highest)
    queries = low(low_back(projected[..., :D] + query_bias)).reshape(window_count, window_area, HEADS, HEAD_DIM)
    key_rows = low(low_back(projected[..., D:2 * D])).reshape(window_count, window_area, HEADS, HEAD_DIM)
    value_rows = low(low_back(projected[..., 2 * D:] + value_bias)).reshape(window_count, window_area, HEADS, HEAD_DIM)
    position = bias_table[relative_index()].transpose(2, 0, 1)
    scores = jnp.einsum('bqhc,bkhc->bhqk', queries, key_rows, precision=highest) * HEAD_DIM ** (-0.5) + position[None]
    if shifted:
        scores = (scores.reshape(page_count, -1, HEADS, window_area, window_area) + shift_mask()[None, :, None]).reshape(scores.shape)
    scores = low_back(scores)
    attention = low(jax.nn.softmax(scores, axis=-1))
    attended = jnp.einsum('bhqk,bkhc->bqhc', attention, value_rows, precision=highest).reshape(window_count, window_area, D)
    attended = low(low_back(attended))
    hidden = tokens + low_back(jnp.einsum('btd,de->bte', attended, proj_weight, precision=highest) + proj_bias)
    normed_two = low(layer_norm(hidden, gain_two, bias_two))
    pre_act = low_back(jnp.einsum('btd,df->btf', normed_two, fc1_weight, precision=highest) + fc1_bias)
    activated = low(jax.nn.gelu(pre_act, approximate=False))
    output = hidden + low_back(jnp.einsum('btf,fd->btd', activated, fc2_weight, precision=highest) + fc2_bias)
    output = from_windows(output, page_count)
    if shifted:
        output = jnp.roll(output, (WINDOW // 2, WINDOW // 2), axis=(1, 2))
    return output

def merge_head(spatial, merge_gain, merge_bias, merge_weight):
    page_count = spatial.shape[0]
    normed = low(layer_norm(patch_merge(spatial), merge_gain, merge_bias))
    column_count = merge_weight.shape[1] // N_PIPE
    halves = []
    for part_index in range(N_PIPE):
        columns = merge_weight[:, part_index * column_count:(part_index + 1) * column_count]
        halves.append(jnp.einsum('nc,co->no', low_back(normed), columns, precision=highest))
    return jnp.concatenate(halves, axis=-1).reshape(page_count, PAGE_H // 2, PAGE_W // 2, -1)

def forward(group_inputs, params):
    block_params, merge_gain, merge_bias, merge_weight = params
    first = swin_block(group_inputs, [stacked[0] for stacked in block_params], False)
    first = low(low_back(first))
    second = swin_block(first, [stacked[1] for stacked in block_params], True)
    return merge_head(second, merge_gain, merge_bias, merge_weight)

def reference(page_inputs, gain_one, bias_one, qkv_weight, query_bias, value_bias, bias_table, proj_weight, proj_bias, gain_two, bias_two, fc1_weight, fc1_bias, fc2_weight, fc2_bias, merge_gain, merge_bias, merge_weight, cotangent):
    block_params = tuple((stacked.astype(jnp.float32) for stacked in (gain_one, bias_one, qkv_weight, query_bias, value_bias, bias_table, proj_weight, proj_bias, gain_two, bias_two, fc1_weight, fc1_bias, fc2_weight, fc2_bias)))
    params = (block_params, merge_gain.astype(jnp.float32), merge_bias.astype(jnp.float32), merge_weight.astype(jnp.float32))
    group_count = PAGES // 2
    grouped_inputs = page_inputs.astype(jnp.float32).reshape(group_count, 2, PAGE_H, PAGE_W, D)
    grouped_cot = cotangent.astype(jnp.float32).reshape(group_count, 2, PAGE_H // 2, PAGE_W // 2, MERGE_OUT)

    def group_step(totals, group_pair):
        group_inputs, group_cot = group_pair
        merged_group, pullback = jax.vjp(forward, group_inputs, params)
        grad_inputs, grad_params = pullback(group_cot)
        return (jax.tree.map(jnp.add, totals, grad_params), (merged_group.astype(jnp.bfloat16), grad_inputs))
    totals, (merged, grad_inputs) = lax.scan(group_step, jax.tree.map(jnp.zeros_like, params), (grouped_inputs, grouped_cot))
    block_grads, grad_merge_gain, grad_merge_bias, grad_merge_weight = totals
    return (merged.reshape(PAGES, PAGE_H // 2, PAGE_W // 2, MERGE_OUT), grad_inputs.reshape(PAGES, PAGE_H, PAGE_W, D), block_grads[0], block_grads[1], block_grads[2], block_grads[3], block_grads[4], block_grads[5], block_grads[6], block_grads[7], block_grads[8], block_grads[9], block_grads[10], block_grads[11], block_grads[12], block_grads[13], grad_merge_gain, grad_merge_bias, grad_merge_weight)
```

```python
import functools

import jax
import jax.numpy as jnp
import numpy as np
from jax import lax
from jax.experimental import pallas as pl
from jax.experimental.pallas import tpu as pltpu
from jax.sharding import PartitionSpec as P

BF = jnp.bfloat16
F32 = jnp.float32
WINDOW = 10
AREA = 100
PAGE = 20
WP = 112
HALO = 304
MROWS = 160
EPS = 1e-05
NEG = -1e30
ROW_TILE = 512


def mm(a, b):
    return lax.dot_general(a, b, (((1,), (0,)), ((), ())), preferred_element_type=F32)


def mm_nt(a, b):
    return lax.dot_general(a, b, (((1,), (1,)), ((), ())), preferred_element_type=F32)


def mm_tn(a, b):
    return lax.dot_general(a, b, (((0,), (0,)), ((), ())), preferred_element_type=F32)


def unit_norm(values):
    centred = values - jnp.mean(values, axis=-1, keepdims=True)
    inv_std = lax.rsqrt(jnp.mean(centred * centred, axis=-1, keepdims=True) + EPS)
    return centred * inv_std, inv_std


def unit_norm_back(grad_normed, unit_rows, inv_std, gain):
    grad_unit = grad_normed * gain
    return inv_std * (
        grad_unit
        - jnp.mean(grad_unit, axis=-1, keepdims=True)
        - unit_rows * jnp.mean(grad_unit * unit_rows, axis=-1, keepdims=True)
    )


def place_tables(pages):
    tokens = pages * 2 * WP
    halo = -(-pages * AREA // 16) * 16
    merged = -(-pages * 50 // 16) * 16
    send0 = np.zeros((halo, tokens), np.float32)
    own1 = np.zeros((tokens, tokens), np.float32)
    halo1 = np.zeros((tokens, halo), np.float32)
    own2 = np.zeros((4 * merged, tokens), np.float32)
    halo2 = np.zeros((4 * merged, halo), np.float32)

    def row0(p, r, col):
        return (p * 2 + col // WINDOW) * WP + r * WINDOW + col % WINDOW

    def row1(p, r, col):
        shifted = (col - 5) % PAGE
        return (p * 2 + shifted // WINDOW) * WP + r * WINDOW + shifted % WINDOW

    def rowh(p, r, col):
        return p * AREA + r * PAGE + col

    for p in range(pages):
        for col in range(PAGE):
            for r in range(5):
                send0[rowh(p, r, col), row0(p, r, col)] = 1
                own1[row1(p, r, col), row0(p, r + 5, col)] = 1
                halo1[row1(p, r + 5, col), rowh(p, r, col)] = 1
        for k in range(4):
            for m in range(5):
                for n in range(10):
                    row = k * merged + p * 50 + m * 10 + n
                    r, col = 2 * m + k % 2, 2 * n + k // 2
                    if r >= 5:
                        own2[row, row1(p, r - 5, col)] = 1
                    else:
                        halo2[row, rowh(p, r, col)] = 1
    return tuple(jnp.asarray(t, BF) for t in (send0, own1, halo1, own2, halo2))


def code_matrices():
    select = np.zeros((WP, 384), np.float32)
    back = np.zeros((184, WP), np.float32)
    for i in range(AREA):
        code = (i // WINDOW) * 19 + i % WINDOW
        select[i, code] = 1
        back[183 - code, i] = 1
    return jnp.asarray(select, BF), jnp.asarray(back, BF)


def expand_table(table, select, pos):
    for h in range(table.shape[0]):
        spread = pltpu.roll(jnp.broadcast_to(table[h : h + 1, :], (184, 384)), 208, 1, stride=1, stride_axis=0)
        rows = mm(select[:, 0:184], spread.astype(BF)).astype(BF)
        pos[h * WP : (h + 1) * WP, :] = mm_nt(rows, select[...]).astype(BF)


def reduce_table(score, select, back, out):
    for h in range(out.shape[0]):
        block = score[h * WP : (h + 1) * WP, :]
        high = block.astype(BF)
        low = (block - high.astype(F32)).astype(BF)
        codes = mm(back[...], mm(high, select[...]).astype(BF)) + mm(back[...], mm(low, select[...]).astype(BF))
        turned = pltpu.roll(codes, 0, 1, stride=1, stride_axis=0)
        out[h : h + 1, 0:384] = jnp.sum(turned, axis=0, keepdims=True)


class Copies:
    def __init__(self, sems):
        self.sems, self.used = sems, 0

    def start(self, source, target):
        copy = pltpu.make_async_copy(source, target, self.sems.at[self.used])
        self.used += 1
        copy.start()
        return copy

    def pick(self, mine, own, other, target):
        copy = pltpu.make_async_copy(own, target, self.sems.at[self.used])
        away = pltpu.make_async_copy(other, target, self.sems.at[self.used])
        self.used += 1

        @pl.when(mine)
        def _():
            copy.start()

        @pl.when(jnp.logical_not(mine))
        def _():
            away.start()

        return copy


def head_masks(kind):
    lane = lax.broadcasted_iota(jnp.int32, (1, 128), 1) // 32
    return [jnp.where(lane == h, 1.0, 0.0).astype(kind) for h in range(4)]


def stack_heads(block, masks):
    return jnp.concatenate([block * mask for mask in masks], axis=0)


def pick_heads(stacked, masks):
    total = stacked[0:WP] * masks[0]
    for h in range(1, 4):
        total = total + stacked[h * WP : (h + 1) * WP] * masks[h]
    return total


def block_forward(x_ref, small, weights, ready, pos, mask, bufs, n_ref, copies, outs):
    qkv, attn, attended, hidden, act, dgelu = bufs
    wqkv, wproj, wfc1, _ = weights
    tokens = x_ref.shape[0]
    sent = []
    unit_one, _ = unit_norm(x_ref[...].astype(F32))
    n_ref[...] = (unit_one * small[0:1] + small[1:2]).astype(BF)
    zero = jnp.zeros((1, 512), F32)
    bias = [small[2:3], zero, small[3:4]]
    ready[0].wait()
    for j in range(6):
        shift = bias[j // 2][:, (j % 2) * 256 : (j % 2) * 256 + 256]
        qkv[:, j * 256 : j * 256 + 256] = (
            mm(n_ref[...], wqkv[:, j * 256 : j * 256 + 256]) + shift
        ).astype(BF)
    sent.append(copies.start(qkv, outs[0]))
    low_masks, masks = head_masks(BF), head_masks(F32)

    def window(w, carry):
        rows = pl.ds(pl.multiple_of(w * WP, 16), WP)
        side = mask[w % 2]
        for blk in range(4):
            q = qkv[rows, blk * 128 : blk * 128 + 128]
            k = qkv[rows, 512 + blk * 128 : 512 + blk * 128 + 128]
            v = qkv[rows, 1024 + blk * 128 : 1024 + blk * 128 + 128]
            s = mm_nt(stack_heads(q, low_masks), k) * 32**-0.5
            s = s + pos[blk * 4 * WP : (blk + 1) * 4 * WP, :].astype(F32)
            s = (s.reshape(4, WP, WP) + side[None]).reshape(4 * WP, WP)
            e = jnp.exp(s - jnp.max(s, axis=-1, keepdims=True))
            a = (e * (1.0 / jnp.sum(e, axis=-1, keepdims=True))).astype(BF)
            attn[pl.ds(pl.multiple_of((w * 4 + blk) * 4 * WP, 16), 4 * WP), :] = a
            attended[rows, blk * 128 : blk * 128 + 128] = pick_heads(mm(a, v), masks).astype(BF)
        return carry

    lax.fori_loop(0, tokens // WP, window, 0)
    sent.append(copies.start(attn, outs[1]))
    sent.append(copies.start(attended, outs[2]))
    ready[1].wait()
    for j in range(2):
        cols = slice(j * 256, j * 256 + 256)
        hidden[:, cols] = x_ref[:, cols].astype(F32) + (mm(attended[...], wproj[:, cols]) + small[4:5, cols])
    sent.append(copies.start(hidden, outs[3]))
    unit_two, _ = unit_norm(hidden[...])
    n_ref[...] = (unit_two * small[5:6] + small[6:7]).astype(BF)
    ready[2].wait()
    for j in range(8):
        cols = slice(j * 256, j * 256 + 256)
        u = mm(n_ref[...], wfc1[:, cols]) + small[8 + j // 2 : 9 + j // 2, (j % 2) * 256 : (j % 2) * 256 + 256]
        cdf = 0.5 + 0.5 * lax.erf(u * (0.5**0.5))
        act[:, cols] = (u * cdf).astype(BF)
        dgelu[:, cols] = (cdf + u * (jnp.exp(u * u * -0.5) * ((2 * np.pi) ** -0.5))).astype(BF)
    sent.append(copies.start(act, outs[4]))
    sent.append(copies.start(dgelu, outs[5]))
    ready[3].wait()
    return sent


def layer_out(bufs, weights, small, out):
    hidden, act = bufs[3], bufs[4]
    for j in range(2):
        cols = slice(j * 256, j * 256 + 256)
        out[:, cols] = (hidden[:, cols] + (mm(act[...], weights[3][:, cols]) + small[7:8, cols])).astype(BF)


def forward0_kernel(x_ref, small, table, select, mask, send0, *refs):
    own, other, outs, out, halo = refs[0:4], refs[4:8], refs[8:14], refs[14], refs[15]
    weights, bufs, pos, n_ref, sems = refs[16:20], refs[20:26], refs[26], refs[27], refs[28]
    copies = Copies(sems)
    mine = lax.axis_index("pipe") == 0
    ready = [copies.pick(mine, a, b, w) for a, b, w in zip(own, other, weights)]
    expand_table(table, select, pos)
    sent = block_forward(x_ref, small, weights, ready, pos, mask, bufs, n_ref, copies, outs)
    layer_out(bufs, weights, small, out)
    halo[...] = mm(send0[...], out[...]).astype(BF)
    for copy in sent:
        copy.wait()


def forward1_kernel(prev, arrived, own1, halo1, small, table, select, mask, *refs):
    own, other, x_ref, outs, out, halo = refs[0:4], refs[4:8], refs[8], refs[9:15], refs[15], refs[16]
    weights, bufs, pos, n_ref, sems = refs[17:21], refs[21:27], refs[27], refs[28], refs[29]
    copies = Copies(sems)
    mine = lax.axis_index("pipe") == 1
    ready = [copies.pick(mine, a, b, w) for a, b, w in zip(own, other, weights)]
    expand_table(table, select, pos)
    x_ref[...] = (mm(own1[...], prev[...]) + mm(halo1[...], arrived[...])).astype(BF)
    sent = block_forward(x_ref, small, weights, ready, pos, mask, bufs, n_ref, copies, outs)
    layer_out(bufs, weights, small, out)
    halo[...] = mm_tn(halo1[...], out[...]).astype(BF)
    for copy in sent:
        copy.wait()


def merge_kernel(own, arrived, own2, halo2, vectors, cot, wm_own, wm_other, merged, parts, grad_small, grad_own, grad_halo,
                 rows_ref, normed, ghead, wm, grad_w, sems):
    copies = Copies(sems)
    mine = lax.axis_index("pipe") == 0
    ready = [copies.pick(mine, wm_own, wm_other, wm.at[0]), copies.pick(mine, wm_other, wm_own, wm.at[1])]
    sent = []
    count = rows_ref.shape[0]
    for k in range(4):
        part = mm(own2[k * count : (k + 1) * count, :], own[...]) + mm(halo2[k * count : (k + 1) * count, :], arrived[...])
        rows_ref[:, k * 512 : k * 512 + 512] = part
    unit, inv_std = unit_norm(rows_ref[...])
    gain = vectors[0:1]
    normed[...] = (unit * gain + vectors[1:2]).astype(BF)
    for half in range(2):
        ready[half].wait()
        merged[half] = mm(normed[...], wm[half]).astype(BF)
        for k in range(4):
            cols = slice(k * 512, k * 512 + 512)
            term = mm_nt(cot[half], wm[half, cols, :]).astype(BF).astype(F32)
            if half == 0:
                ghead[:, cols] = term
            else:
                ghead[:, cols] = ghead[:, cols] + term
            grad_w[half, cols, :] = mm_tn(normed[:, cols], cot[half]).astype(BF)
        sent.append(copies.start(grad_w.at[half], parts.at[half, 6144:8192]))
    grad = ghead[...]
    over_rows = [jnp.sum(grad * unit, axis=0, keepdims=True), jnp.sum(grad, axis=0, keepdims=True)]
    for i in range(2):
        for k in range(4):
            grad_small[i * 4 + k : i * 4 + k + 1] = over_rows[i][:, k * 512 : k * 512 + 512]
    grad_rows = unit_norm_back(grad, unit, inv_std, gain).astype(BF)
    stacked = jnp.concatenate([grad_rows[:, k * 512 : k * 512 + 512] for k in range(4)], axis=0)
    grad_own[...] = mm_tn(own2[...], stacked)
    grad_halo[...] = mm_tn(halo2[...], stacked).astype(BF)
    for copy in sent:
        copy.wait()


def block_backward(layer, g_ref, x_ref, small, select, back, merge_sums, sources, mine, own, other, parts, refs):
    weights, bufs, gm, gpre, n_ref, dqkv, work, score_sum, grad_small, grad_w, tail, sems = refs
    wqkv, wproj, wfc1, wfc2 = weights
    qkv, attn, attended, hidden, act, dgelu = bufs
    copies = Copies(sems)
    got = {}

    def fetch(name, source, target):
        got[name] = copies.start(source, target)

    def fetch_weight(name, i):
        got[name] = copies.pick(mine, own[i], other[i], weights[i])

    fetch("act", sources[4], act)
    fetch_weight("fc2", 3)
    fetch("dgelu", sources[5], dgelu)
    fetch("hidden", sources[3], hidden)
    fetch_weight("fc1", 2)
    fetch("attended", sources[2], attended)
    fetch_weight("proj", 1)
    fetch("qkv", sources[0], qkv)
    fetch("attn", sources[1], attn)
    fetch_weight("wqkv", 0)
    tokens = g_ref.shape[0]
    sent = []

    def send(start, stop):
        sent.append(copies.start(grad_w.at[start:stop], parts.at[layer, start:stop]))

    def put(row, value):
        grad_small[row : row + 1] = jnp.sum(value, axis=0, keepdims=True)

    grad_small[...] = jnp.zeros_like(grad_small)
    gm[...] = g_ref[...].astype(BF)
    put(7, gm[...].astype(F32))
    got["act"].wait()
    got["fc2"].wait()
    got["dgelu"].wait()
    for j in range(8):
        cols = slice(j * 256, j * 256 + 256)
        grad_w[4096 + j * 256 : 4096 + j * 256 + 256, :] = mm_tn(act[:, cols], gm[...]).astype(BF)
        d = mm_nt(gm[...], wfc2[cols, :]) * dgelu[:, cols].astype(F32)
        low = d.astype(BF)
        gpre[:, cols] = low
        grad_small[8 + j // 2 : 9 + j // 2, (j % 2) * 256 : (j % 2) * 256 + 256] = jnp.sum(
            low.astype(F32), axis=0, keepdims=True
        )
    send(4096, 6144)
    got["hidden"].wait()
    unit, inv_std = unit_norm(hidden[...])
    n_ref[...] = (unit * small[5:6] + small[6:7]).astype(BF)
    for b in range(4):
        grad_w[2048 + b * 512 : 2048 + b * 512 + 512, :] = mm_tn(n_ref[...], gpre[:, b * 512 : b * 512 + 512]).astype(BF)
    send(2048, 4096)
    got["fc1"].wait()
    for j in range(2):
        work[:, j * 256 : j * 256 + 256] = mm_nt(gpre[...], wfc1[j * 256 : j * 256 + 256, :])
    dn = work[...]
    put(5, dn * unit)
    put(6, dn)
    g_ref[...] = g_ref[...] + unit_norm_back(dn, unit, inv_std, small[5:6])
    gm[...] = g_ref[...].astype(BF)
    put(4, gm[...].astype(F32))
    got["attended"].wait()
    grad_w[1536:2048, :] = mm_tn(attended[...], gm[...]).astype(BF)
    send(1536, 2048)
    got["proj"].wait()
    for j in range(2):
        n_ref[:, j * 256 : j * 256 + 256] = mm_nt(gm[...], wproj[j * 256 : j * 256 + 256, :]).astype(BF)
    low_masks, masks = head_masks(BF), head_masks(F32)
    score_sum[...] = jnp.zeros_like(score_sum)
    got["qkv"].wait()
    got["attn"].wait()

    def window(w, carry):
        rows = pl.ds(pl.multiple_of(w * WP, 16), WP)
        for blk in range(4):
            q = qkv[rows, blk * 128 : blk * 128 + 128]
            k = qkv[rows, 512 + blk * 128 : 512 + blk * 128 + 128]
            v = qkv[rows, 1024 + blk * 128 : 1024 + blk * 128 + 128]
            go = stack_heads(n_ref[rows, blk * 128 : blk * 128 + 128], low_masks)
            a = attn[pl.ds(pl.multiple_of((w * 4 + blk) * 4 * WP, 16), 4 * WP), :]
            p = mm_nt(go, v)
            wide = a.astype(F32)
            ap = wide * p
            ds = ap - wide * jnp.sum(ap, axis=-1, keepdims=True)
            low = ds.astype(BF)
            score_sum[blk * 4 * WP : (blk + 1) * 4 * WP, :] += low.astype(F32)
            dqkv[rows, 1024 + blk * 128 : 1024 + blk * 128 + 128] = mm_tn(a, go).astype(BF)
            dqkv[rows, blk * 128 : blk * 128 + 128] = (pick_heads(mm(low, k), masks) * 32**-0.5).astype(BF)
            dqkv[rows, 512 + blk * 128 : 512 + blk * 128 + 128] = (
                mm_tn(low, stack_heads(q, low_masks)) * 32**-0.5
            ).astype(BF)
        return carry

    lax.fori_loop(0, tokens // WP, window, 0)
    unit, inv_std = unit_norm(x_ref[...].astype(F32))
    n_ref[...] = (unit * small[0:1] + small[1:2]).astype(BF)
    for b in range(3):
        grad_w[b * 512 : b * 512 + 512, :] = mm_tn(n_ref[...], dqkv[:, b * 512 : b * 512 + 512]).astype(BF)
    send(0, 1536)
    put(2, dqkv[:, 0:512].astype(F32))
    put(3, dqkv[:, 1024:1536].astype(F32))
    got["wqkv"].wait()
    for j in range(2):
        work[:, j * 256 : j * 256 + 256] = mm_nt(dqkv[...], wqkv[j * 256 : j * 256 + 256, :])
    dn = work[...]
    put(0, dn * unit)
    put(1, dn)
    reduce_table(score_sum, select, back, grad_small.at[16:32])
    grad_small[32:40] = merge_sums[...]
    tail[...] = jnp.zeros_like(tail)
    tail[0:48] = grad_small[...].astype(BF)
    sent.append(copies.start(tail, parts.at[layer, 8192:]))
    g_ref[...] = g_ref[...] + unit_norm_back(dn, unit, inv_std, small[0:1])
    return sent


def backward1_kernel(grad_own, arrived, own1, halo1, x_ref, small, select, back, merge_sums, *refs):
    sources, own, other, _, parts, grad_prev, grad_halo, g_ref = refs[0:6], refs[6:10], refs[10:14], refs[14], *refs[15:19]
    rest = refs[19:]
    gm = rest[10]
    g_ref[...] = grad_own[...] + mm(halo1[...], arrived[...])
    mine = lax.axis_index("pipe") == 1
    sent = block_backward(1, g_ref, x_ref, small, select, back, merge_sums, sources, mine, own, other, parts,
                          (rest[0:4], rest[4:10], *rest[10:]))
    gm[...] = g_ref[...].astype(BF)
    grad_prev[...] = mm_tn(own1[...], gm[...])
    grad_halo[...] = mm_tn(halo1[...], gm[...]).astype(BF)
    for copy in sent:
        copy.wait()


def backward0_kernel(grad_own, arrived, send0, x_ref, small, select, back, merge_sums, *refs):
    sources, own, other, _, parts, g_ref = refs[0:6], refs[6:10], refs[10:14], refs[14], *refs[15:17]
    rest = refs[17:]
    g_ref[...] = grad_own[...] + mm_tn(send0[...], arrived[...])
    mine = lax.axis_index("pipe") == 0
    sent = block_backward(0, g_ref, x_ref, small, select, back, merge_sums, sources, mine, own, other, parts,
                          (rest[0:4], rest[4:10], *rest[10:]))
    for copy in sent:
        copy.wait()


def widen_kernel(total, wqkv, wproj, wfc1, wfc2, wmerge, tail, rows, stage, load_sem, store_sem):
    blocks = []
    for b in range(3):
        blocks.append((b * 512, wqkv.at[:, b * 512 : b * 512 + 512]))
    blocks.append((1536, wproj))
    for b in range(4):
        blocks.append((2048 + b * 512, wfc1.at[:, b * 512 : b * 512 + 512]))
    for b in range(4):
        blocks.append((4096 + b * 512, wfc2.at[b * 512 : b * 512 + 512, :]))
    for b in range(4):
        blocks.append((6144 + b * 512, wmerge.at[b * 512 : b * 512 + 512, :]))
    loads = []
    for i, (start, _) in enumerate(blocks + [(8192, None)]):
        count = min(512, total.shape[0] - start)
        copy = pltpu.make_async_copy(total.at[start : start + count], rows.at[start : start + count], load_sem.at[i])
        copy.start()
        loads.append(copy)
    stores = []
    for i, (start, target) in enumerate(blocks):
        slot = i % 4
        loads[i].wait()
        if i >= 4:
            stores[i - 4].wait()
        stage[slot] = rows[start : start + 512, :].astype(F32)
        copy = pltpu.make_async_copy(stage.at[slot], target, store_sem.at[slot])
        copy.start()
        stores.append(copy)
    loads[-1].wait()
    tail[...] = rows[8192:8240, :].astype(F32)
    for copy in stores[-4:]:
        copy.wait()


HBM = pl.BlockSpec(memory_space=pl.ANY)
VMEM = pl.BlockSpec(memory_space=pltpu.VMEM)


def call(kernel, args, outs, scratch, name, aliases=None):
    return pl.pallas_call(
        kernel,
        out_shape=[jax.ShapeDtypeStruct(s, d) for s, d, _ in outs],
        in_specs=[spec for _, spec in args],
        out_specs=[spec for _, _, spec in outs],
        scratch_shapes=[pltpu.SemaphoreType.DMA((s,)) if isinstance(s, int) else pltpu.VMEM(*s) for s in scratch],
        compiler_params=pltpu.CompilerParams(vmem_limit_bytes=60 * 1024 * 1024),
        input_output_aliases=aliases or {},
        name=name,
    )(*[value for value, _ in args])


def other_core(value):
    return lax.ppermute(value, "pipe", [(0, 1), (1, 0)])


def shift_masks(core):
    place = jnp.arange(WP, dtype=jnp.int32)
    pad = jnp.where(place < AREA, 0.0, NEG).astype(F32)
    row_late = ((place // WINDOW) >= 5) & (core == 1)
    masks = []
    for side in range(2):
        late = row_late.astype(jnp.int32) * 2 + (((place % WINDOW) >= 5) & (side == 1)).astype(jnp.int32)
        masks.append(jnp.where(late[:, None] != late[None, :], -100.0, 0.0).astype(F32) + pad[None, :])
    plain = jnp.broadcast_to(pad[None, None, :], (2, WP, WP))
    return plain, jnp.stack(masks)


MESH = pl.DeviceIdType.MESH
ORDERS = ((0, 1, 2), (1, 0, 2), (2, 0, 1))


def dp_axes(dp):
    bits=dp.bit_length()-1
    b0=bits//3; b1=(bits-b0)//2; b2=bits-b0-b1
    sizes=[1<<b0,1<<b1,1<<b2]
    return [(1,sizes[0]),(sizes[0],sizes[1]),(sizes[0]*sizes[1],sizes[2])]

ORDERS=((0,1,2),(1,0,2),(2,0,1))

class Line:
    def __init__(self, me, stride, size):
        self.size=size; self.pos=lax.rem(me // stride, size); self.up=me+stride; self.down=me-stride

def plan(dp, chunk):
    axes=dp_axes(dp); plans=[]; most=0
    for order in ORDERS:
        events=[]; length=chunk; slot=0
        for k,a in enumerate(order):
            n=axes[a][1]; piece=length//n
            for s in range(1,n):
                events.append(("rs",k,s,piece,slot)); slot+=2*piece if n>2 else piece
            length=piece
        for k in (2,1,0):
            a=order[k]; n=axes[a][1]
            piece=length
            for s in range(1,n):
                events.append(("ag",k,s,piece,0))
            length*=n
        plans.append(events); most=max(most,slot)
    return axes,plans,most

def comm_kernel(dp, nchunk, chunk, parts, out_hbm, acc, paired, slots, pair_send, pair_recv, load_sem, store_sem, send_sem, recv_sem):
    core=lax.axis_index("pipe"); me=lax.axis_index("dp")
    axes,plans,slot_rows=plan(dp,chunk)
    lines=[Line(me,st,n) for st,n in axes]
    partner=1-core
    barrier=pltpu.get_barrier_semaphore()
    pl.semaphore_signal(barrier,inc=1,device_id=(partner,me),device_id_type=MESH)
    expect=jnp.int32(1)
    for ln in lines:
        @pl.when(ln.pos>0)
        def _(): pl.semaphore_signal(barrier,inc=1,device_id=(core,ln.down),device_id_type=MESH)
        @pl.when(ln.pos<ln.size-1)
        def _(): pl.semaphore_signal(barrier,inc=1,device_id=(core,ln.up),device_id_type=MESH)
        expect=expect+jnp.where(ln.pos>0,1,0)+jnp.where(ln.pos<ln.size-1,1,0)
    pl.semaphore_wait(barrier,expect)

    def rows(start,count): return pl.ds(pl.multiple_of(start,16),count)
    def pair_copy(q):
        r=rows(q*chunk,chunk)
        return pltpu.make_async_remote_copy(src_ref=parts.at[partner, r],dst_ref=paired.at[r],send_sem=pair_send.at[q],recv_sem=pair_recv.at[q],device_id=(partner,me),device_id_type=MESH)
    def load(q):
        r=rows(q*chunk,chunk)
        return pltpu.make_async_copy(parts.at[core, r],acc.at[r],load_sem.at[q])
    def store(q):
        r=rows(q*chunk,chunk)
        return pltpu.make_async_copy(paired.at[r],out_hbm.at[r],store_sem.at[q])
    def begin(q,c):
        pair_copy(q).start(); load(q).start(); return c
    lax.fori_loop(0,nchunk,begin,0)

    def moves(q,kind,e):
        order=ORDERS[kind]; what,k,s,piece,slot=plans[kind][e]
        base=q*chunk; length=chunk
        for i in range(k):
            ln=lines[order[i]]; length=length//ln.size; base=base+ln.pos*length
        ln=lines[order[k]]; n=ln.size; p=ln.pos
        result=[]
        for d in range(2):
            ahead=ln.up if d==0 else ln.down
            mirrored=p if d==0 else n-1-p
            if what=="rs":
                sends=mirrored<=s-1; gets=jnp.logical_and(mirrored>=1,mirrored<=s)
                piece_of=p+n-s if d==0 else p-n+s
                piece_of=jnp.clip(piece_of,0,n-1)
                source=rows(base+piece_of*piece,piece)
                place=slot+(d*piece if n>2 else 0)
                target=rows(q*slot_rows+place,piece)
                next_of=p+n-s-1 if d==0 else p-n+s+1
                into=rows(base+jnp.clip(next_of,0,n-1)*piece,piece)
                copy=pltpu.make_async_remote_copy(src_ref=acc.at[source],dst_ref=slots.at[target],send_sem=send_sem.at[q,e,d],recv_sem=recv_sem.at[q,e,d],device_id=(core,ahead),device_id_type=MESH)
                result.append((sends,gets,copy,target,into))
            else:
                sends=jnp.logical_and(mirrored<n-1,mirrored>=s-1); gets=mirrored>=s
                piece_of=p-s+1 if d==0 else p+s-1
                source=rows(base+jnp.clip(piece_of,0,n-1)*piece,piece)
                copy=pltpu.make_async_remote_copy(src_ref=paired.at[source],dst_ref=paired.at[source],send_sem=send_sem.at[q,e,d],recv_sem=recv_sem.at[q,e,d],device_id=(core,ahead),device_id_type=MESH)
                result.append((sends,gets,copy,None,None))
        return result

    def finish(q,kind,e):
        for sends,gets,copy,target,into in moves(q,kind,e):
            @pl.when(gets)
            def _():
                copy.wait_recv()
                if into is not None:
                    acc[into,:]=(acc[into,:].astype(F32)+slots[target,:].astype(F32)).astype(BF)
            @pl.when(sends)
            def _():
                copy.wait_send()
    def event(q,kind,e):
        events=plans[kind]
        if e==0:
            load(q).wait(); pair_copy(q).wait()
            def add(i,c):
                r=rows(q*chunk+i*64,64)
                acc[r,:]=(acc[r,:].astype(F32)+paired[r,:].astype(F32)).astype(BF)
                return c
            lax.fori_loop(0,chunk//64,add,0)
        else:
            finish(q,kind,e-1)
        if e<len(events):
            if events[e][0]=="ag" and events[e-1][0]=="rs":
                base=q*chunk; length=chunk
                for a in ORDERS[kind]:
                    ln=lines[a]; length=length//ln.size; base=base+ln.pos*length
                r=rows(base,length)
                paired[r,:]=acc[r,:]
            for sends,gets,copy,target,into in moves(q,kind,e):
                @pl.when(sends)
                def _(): copy.start()
        else:
            store(q).start()
    count=len(plans[0])+1
    groups=-(-nchunk//3)
    def tick(t,c):
        for e in reversed(range(count)):
            j=t-e
            for kind in range(3):
                q=j*3+kind
                @pl.when(jnp.logical_and(j>=0,q<nchunk))
                def _(): event(q,kind,e)
        return c
    lax.fori_loop(0,groups+(count-1),tick,0)
    def end(q,c):
        store(q).wait(); return c
    lax.fori_loop(0,nchunk,end,0)

def sum_rows(parts, dp, chunk):
    rows = parts.shape[1]
    count = rows // chunk
    _, plans, slot_rows = plan(dp, chunk)
    events = len(plans[0])
    dma = pltpu.SemaphoreType.DMA
    return pl.pallas_call(
        functools.partial(comm_kernel, dp, count, chunk),
        out_shape=jax.ShapeDtypeStruct((rows, 512), BF),
        in_specs=[HBM],
        out_specs=HBM,
        scratch_shapes=[pltpu.VMEM((rows, 512), BF), pltpu.VMEM((rows, 512), BF), pltpu.VMEM((count * slot_rows, 512), BF),
                        dma((count,)), dma((count,)), dma((count,)), dma((count,)),
                        dma((count, events, 2)), dma((count, events, 2))],
        compiler_params=pltpu.CompilerParams(collective_id=0, has_side_effects=True, vmem_limit_bytes=60 * 1024 * 1024),
        name="sum_rows",
    )(parts)


def shards(
    page_inputs, gain_one, bias_one, qkv_weight, query_bias, value_bias, bias_table, proj_weight, proj_bias,
    gain_two, bias_two, fc1_weight, fc1_bias, fc2_weight, fc2_bias, merge_gain, merge_bias, merge_weight, cotangent,
):
    dp = lax.axis_size("dp")
    core = lax.axis_index("pipe")
    pages = page_inputs.shape[0]
    tokens = pages * 2 * WP
    heads = bias_table.shape[2]
    table = bias_table.shape[1]
    send0, own1, halo1, own2, halo2 = place_tables(pages)
    halo_rows, merged_rows = send0.shape[0], own2.shape[0] // 4

    def both(own):
        other = other_core(own)
        return [jnp.where(core == 0, own, other), jnp.where(core == 0, other, own)]

    mine = lax.dynamic_slice_in_dim(page_inputs, core * 10, 10, axis=1)
    yours = lax.dynamic_slice_in_dim(page_inputs, (1 - core) * 10, 10, axis=1)
    yours = other_core(yours)
    rows = jnp.concatenate([jnp.where(core == 0, mine, yours), jnp.where(core == 0, yours, mine)], axis=-1)
    rows = rows.reshape(pages, 10, 2, 10, 512).transpose(0, 2, 1, 3, 4).reshape(pages * 2, AREA, 512)
    x0 = jnp.pad(rows, ((0, 0), (0, WP - AREA), (0, 0))).reshape(tokens, 512)

    small_own = jnp.concatenate(
        [gain_one, bias_one, query_bias, value_bias, proj_bias, gain_two, bias_two, fc2_bias,
         fc1_bias.reshape(4, 512), jnp.zeros((4, 512), BF)], axis=0)
    small = [s.astype(F32) for s in both(small_own)]
    turned = jnp.pad(bias_table[0].T[:, ::-1], ((0, 0), (0, 384 - table)))
    tables = [t.astype(F32) for t in both(jnp.roll(turned, -4, axis=1))]
    select, back = code_matrices()
    masks = shift_masks(core)
    own = [qkv_weight[0], proj_weight[0], fc1_weight[0], fc2_weight[0]]
    other = [other_core(w) for w in own]
    wm_other = other_core(merge_weight)
    stacks = [(w, HBM) for w in own + other]

    cmine = lax.dynamic_slice_in_dim(cotangent, core * 5, 5, axis=1)
    cyours = other_core(lax.dynamic_slice_in_dim(cotangent, (1 - core) * 5, 5, axis=1))
    cot = jnp.stack([jnp.where(core == 0, cmine, cyours), jnp.where(core == 0, cyours, cmine)])
    cot = jnp.pad(cot.reshape(2, pages * 50, 512), ((0, 0), (0, merged_rows - pages * 50), (0, 0)))

    def at(spec, *values):
        return [(v, spec) for v in values]

    saved_shapes = [((tokens, 1536), BF), ((pages * 2 * heads * WP, WP), BF), ((tokens, 512), BF), ((tokens, 512), F32),
                    ((tokens, 2048), BF), ((tokens, 2048), BF)]
    saved_out = [(*shape, HBM) for shape in saved_shapes]
    weight_shapes = [(w.shape, BF) for w in own]
    rows = ((tokens, 512), BF)
    wide_rows = ((tokens, 512), F32)
    halo = ((halo_rows, 512), BF)
    scratch = weight_shapes + saved_shapes + [((heads * WP, WP), BF), rows, 10]
    *saved0, out0, send = call(
        forward0_kernel, at(VMEM, x0, small[0], tables[0], select, masks[0], send0) + stacks,
        saved_out + [(*rows, VMEM), (*halo, VMEM)], scratch, "layer_zero")
    arrived = other_core(send)
    x1, *saved1, out1, send = call(
        forward1_kernel, at(VMEM, out0, arrived, own1, halo1, small[1], tables[1], select, masks[1]) + stacks,
        [(*rows, VMEM)] + saved_out + [(*rows, VMEM), (*halo, VMEM)], scratch, "layer_one")
    arrived = other_core(send)
    vectors = jnp.stack([merge_gain, merge_bias]).astype(F32)
    chunk = 768 if 768 % (dp * 16) == 0 else dp * 16
    total_rows = 6144 + -(-(2048 + 48) // chunk) * chunk
    merged, parts, merge_sums, grad_own, send = call(
        merge_kernel, at(VMEM, out1, arrived, own2, halo2, vectors, cot) + at(HBM, merge_weight, wm_other),
        [((2, merged_rows, 512), BF, VMEM), ((2, total_rows, 512), BF, HBM), ((8, 512), F32, VMEM), (*wide_rows, VMEM), (*halo, VMEM)],
        [((merged_rows, 2048), F32), ((merged_rows, 2048), BF), ((merged_rows, 2048), F32),
         ((2, 2048, 512), BF), ((2, 2048, 512), BF), 4], "merge")
    arrived = other_core(send)
    work = weight_shapes + saved_shapes + [
        rows, ((tokens, 2048), BF), rows, ((tokens, 1536), BF), wide_rows, ((heads * WP, WP), F32), ((48, 512), F32),
        ((6144, 512), BF), ((total_rows - 8192, 512), BF), 16]
    parts, grad_own, send, _ = call(
        backward1_kernel,
        at(VMEM, grad_own, arrived, own1, halo1, x1, small[1], select, back, merge_sums) + at(HBM, *saved1) + stacks + at(HBM, parts),
        [((2, total_rows, 512), BF, HBM), (*wide_rows, VMEM), (*halo, VMEM), (*wide_rows, VMEM)], work, "layer_one_back", {23: 0})
    arrived = other_core(send)
    parts, grad_x = call(
        backward0_kernel,
        at(VMEM, grad_own, arrived, send0, x0, small[0], select, back, merge_sums) + at(HBM, *saved0) + stacks + at(HBM, parts),
        [((2, total_rows, 512), BF, HBM), (*wide_rows, VMEM)], work, "layer_zero_back", {22: 0})

    grad_x = grad_x.reshape(pages * 2, WP, 512)[:, :AREA].reshape(pages, 2, 10, 10, 512)
    grad_x = grad_x.transpose(0, 2, 1, 3, 4).reshape(pages, 10, PAGE, 512)
    mine = lax.dynamic_slice_in_dim(grad_x, core * 256, 256, axis=3)
    yours = other_core(lax.dynamic_slice_in_dim(grad_x, (1 - core) * 256, 256, axis=3).astype(BF)).astype(F32)
    grad_pages = jnp.where(core == 0, jnp.concatenate([mine, yours], axis=1), jnp.concatenate([yours, mine], axis=1))

    merged = merged[:, : pages * 50].reshape(2, pages, 5, 10, 512)
    mine = lax.dynamic_index_in_dim(merged, core, 0, keepdims=False)
    yours = other_core(lax.dynamic_index_in_dim(merged, 1 - core, 0, keepdims=False))
    merged = jnp.where(core == 0, jnp.concatenate([mine, yours], axis=1), jnp.concatenate([yours, mine], axis=1))

    total = sum_rows(parts, dp, chunk)
    g_qkv, g_proj, g_fc1, g_fc2, g_merge, tail = call(
        widen_kernel, at(HBM, total),
        [((512, 1536), F32, HBM), ((512, 512), F32, HBM), ((512, 2048), F32, HBM), ((2048, 512), F32, HBM),
         ((2048, 512), F32, HBM), ((48, 512), F32, VMEM)],
        [((total_rows, 512), BF), ((4, 512, 512), F32), 17, 4], "widen")
    grad_table = tail[16:32, 3 : 3 + table][:, ::-1].T[None]
    return (
        merged, grad_pages, tail[0:1], tail[1:2], g_qkv[None], tail[2:3], tail[3:4], grad_table,
        g_proj[None], tail[4:5], tail[5:6], tail[6:7], g_fc1[None], tail[8:12].reshape(1, 2048),
        g_fc2[None], tail[7:8], tail[32:36].reshape(2048), tail[36:40].reshape(2048), g_merge,
    )


def solution(mesh):
    row, mat = P("pipe", None), P("pipe", None, None)
    wide = P("dp", None, None, "pipe")
    in_specs = (wide, row, row, mat, row, row, mat, mat, row, row, row, mat, row, mat, row, P(), P(), P(None, "pipe"), wide)
    out_specs = (wide, wide, row, row, mat, row, row, mat, mat, row, row, row, mat, row, mat, row, P(), P(), P(None, "pipe"))
    return jax.shard_map(shards, mesh=mesh, in_specs=in_specs, out_specs=out_specs, check_vma=False)
```

```python
from functools import partial

import jax
import jax.numpy as jnp
import numpy as np
from jax import lax
from jax.experimental import pallas as pl
from jax.experimental.pallas import tpu as pltpu
from jax.sharding import PartitionSpec as P

BF = jnp.bfloat16
F32 = jnp.float32
WINDOW = 10
AREA = 100
PAGE = 20
WP = 112
EPS = 1e-05
NEG = -1e30
MESH = pl.DeviceIdType.MESH
CHIPS = 16
STEPS = 8
UNIT = 256
CHUNK = 768
ROWS = 8448
SLOT = CHUNK + CHUNK // 8
RING = 4
VMEM_LIMIT = 62 * 1024 * 1024
EMITS = [(r, r + 512) for r in range(0, 8192, 512)] + [(8192, 8448)]
KINDS = (0, 2, 0, 1, 1, 3, 1, 0, 0, 1, 2)
SCHEDULE = (
    ((1, 3, 6, 8, 9, 10, 12, 15, 17), (1, 3, 6, 8, 9, 10, 12, 15, 17), (14, 16, 18, 21, 23, 30, 36, 46, 56), (14, 16, 18, 22, 28, 32, 38, 46, 56), (15, 17, 19, 25, 31, 35, 44, 53, 59), (16, 21, 27, 34, 37, 41, 48, 55, 61), (16, 21, 27, 34, 37, 42, 50, 57, 63), (16, 21, 27, 34, 39, 45, 51, 57, 63), (20, 26, 33, 38, 43, 49, 54, 60, 64), (20, 26, 33, 40, 47, 52, 58, 62, 65), (24, 29, 36, 40, 47, 52, 58, 62, 66)),
    ((1, 4, 6, 7, 8, 9, 10, 12, 16), (1, 4, 6, 7, 8, 9, 10, 12, 16), (2, 5, 7, 9, 10, 13, 16, 18, 23), (2, 5, 7, 9, 10, 13, 16, 18, 23), (3, 6, 8, 9, 10, 13, 17, 18, 25), (4, 6, 8, 9, 10, 13, 17, 20, 28), (4, 7, 9, 10, 14, 16, 18, 24, 31), (4, 7, 9, 11, 14, 16, 19, 29, 31), (9, 11, 14, 17, 18, 21, 30, 34, 38), (9, 11, 14, 18, 22, 27, 33, 36, 39), (10, 13, 17, 18, 26, 32, 35, 37, 40)),
)
FALLBACK = (((19,),) * 11, ((19,),) * 11)


def mm(a, b):
    return lax.dot_general(a, b, (((1,), (0,)), ((), ())), preferred_element_type=F32)


def mm_nt(a, b):
    return lax.dot_general(a, b, (((1,), (1,)), ((), ())), preferred_element_type=F32)


def mm_tn(a, b):
    return lax.dot_general(a, b, (((0,), (0,)), ((), ())), preferred_element_type=F32)


def unit_norm(values):
    centred = values - jnp.mean(values, axis=-1, keepdims=True)
    inv_std = lax.rsqrt(jnp.mean(centred * centred, axis=-1, keepdims=True) + EPS)
    return centred * inv_std, inv_std


def unit_norm_back(grad_normed, unit_rows, inv_std, gain):
    grad_unit = grad_normed * gain
    return inv_std * (
        grad_unit
        - jnp.mean(grad_unit, axis=-1, keepdims=True)
        - unit_rows * jnp.mean(grad_unit * unit_rows, axis=-1, keepdims=True)
    )


def place_tables(pages):
    merged = -(-pages * 50 // 16) * 16
    group = -(-pages // 4) * 4
    cots = AREA * group
    take = np.zeros((2, 2 * WP, 400), np.float32)
    pick = np.zeros((2, merged, cots), np.float32)
    send0 = np.zeros((WP, 2 * WP), np.float32)
    own1 = np.zeros((2 * WP, 2 * WP), np.float32)
    halo1 = np.zeros((2 * WP, WP), np.float32)
    own2 = np.zeros((4 * merged, pages * 2 * WP), np.float32)
    halo2 = np.zeros((4 * merged, pages * WP), np.float32)

    def row0(r, col):
        return col // WINDOW * WP + r * WINDOW + col % WINDOW

    def row1(r, col):
        return row0(r, (col - 5) % PAGE)

    for col in range(PAGE):
        for r in range(10):
            for core in range(2):
                take[core, row0(r, col), (core * 10 + r) * PAGE + col] = 1
        for r in range(5):
            send0[r * PAGE + col, row0(r, col)] = 1
            own1[row1(r, col), row0(r + 5, col)] = 1
            halo1[row1(r + 5, col), r * PAGE + col] = 1
    for p in range(pages):
        for m in range(5):
            for n in range(10):
                for core in range(2):
                    pick[core, p * 50 + m * 10 + n, ((core * 5 + m) * 10 + n) * group + p] = 1
                for k in range(4):
                    row = k * merged + p * 50 + m * 10 + n
                    r, col = 2 * m + k % 2, 2 * n + k // 2
                    if r >= 5:
                        own2[row, p * 2 * WP + row1(r - 5, col)] = 1
                    else:
                        halo2[row, p * WP + r * PAGE + col] = 1
    return {name: jnp.asarray(t, BF) for name, t in dict(
        take=take, back=take.transpose(0, 2, 1), pick=pick, send0=send0, own1=own1, halo1=halo1, own2=own2, halo2=halo2).items()}


def window_masks():
    place = np.arange(WP)
    pad = np.where(place < AREA, 0.0, NEG)
    masks = np.zeros((3, 2, WP, WP), np.float32)
    for kind in range(3):
        for side in range(2):
            late = (place // WINDOW >= 5) * 2 * (kind == 2) + (place % WINDOW >= 5) * (side == 1) * (kind > 0)
            masks[kind, side] = np.where(late[:, None] != late[None, :], -100.0, 0.0) + pad[None, :]
    return jnp.asarray(masks)


def by_page(pages, matrix, rows):
    count = matrix.shape[1]
    return jnp.concatenate([mm(matrix[...], rows[p * count : (p + 1) * count]) for p in range(pages)], axis=0)


def by_page_back(pages, matrix, rows):
    count = matrix.shape[0]
    return jnp.concatenate([mm_tn(matrix[...], rows[p * count : (p + 1) * count]) for p in range(pages)], axis=0)


def code_matrices():
    select = np.zeros((WP, 384), np.float32)
    back = np.zeros((184, WP), np.float32)
    for i in range(AREA):
        code = (i // WINDOW) * 19 + i % WINDOW
        select[i, code] = 1
        back[183 - code, i] = 1
    return jnp.asarray(select, BF), jnp.asarray(back, BF)


def expand_table(table, select, pos):
    entries = table[...].astype(F32)
    for h in range(table.shape[0]):
        spread = pltpu.roll(jnp.broadcast_to(entries[h : h + 1, :], (184, 384)), 208, 1, stride=1, stride_axis=0)
        rows = mm(select[:, 0:184], spread.astype(BF)).astype(BF)
        pos[h * WP : (h + 1) * WP, :] = mm_nt(rows, select[...]).astype(BF)


def reduce_table(score, select, back, out):
    for h in range(out.shape[0]):
        block = score[h * WP : (h + 1) * WP, :].astype(BF)
        codes = mm(back[...], mm(block, select[:, 0:256]).astype(BF))
        codes = jnp.concatenate([codes, jnp.zeros((184, 128), F32)], axis=1)
        turned = pltpu.roll(codes, 0, 1, stride=1, stride_axis=0)
        out[h : h + 1, 0:384] = jnp.sum(turned, axis=0, keepdims=True)


def head_masks(kind):
    lane = lax.broadcasted_iota(jnp.int32, (1, 128), 1) // 32
    return [jnp.where(lane == h, 1.0, 0.0).astype(kind) for h in range(4)]


def stack_heads(block, masks):
    return jnp.concatenate([block * mask for mask in masks], axis=0)


def pick_heads(stacked, masks):
    total = stacked[0:WP] * masks[0]
    for h in range(1, 4):
        total = total + stacked[h * WP : (h + 1) * WP] * masks[h]
    return total


def block_forward(x_ref, small, weights, ready, pos, mask, bufs, n_ref, keep, free):
    qkv, attn, attended, hidden, act, dgelu = bufs
    wqkv, wproj, wfc1, _ = weights
    tokens = x_ref.shape[0]
    unit_one, _ = unit_norm(x_ref[...].astype(F32))
    n_ref[...] = (unit_one * small[0:1] + small[1:2]).astype(BF)
    zero = jnp.zeros((1, 512), F32)
    bias = [small[2:3], zero, small[3:4]]
    ready(0)
    free(0)
    for j in range(6):
        shift = bias[j // 2][:, (j % 2) * 256 : (j % 2) * 256 + 256]
        qkv[:, j * 256 : j * 256 + 256] = (mm(n_ref[...], wqkv[:, j * 256 : j * 256 + 256]) + shift).astype(BF)
    keep(0)
    free(1)
    free(2)
    low_masks, masks = head_masks(BF), head_masks(F32)

    def window(w, carry):
        rows = aligned(w * WP, WP)
        side = mask[w % 2]
        for blk in range(4):
            q, k, v = [qkv[rows, i * 512 + blk * 128 : i * 512 + blk * 128 + 128] for i in range(3)]
            s = mm_nt(stack_heads(q, low_masks), k) * 32**-0.5
            s = s + pos[blk * 4 * WP : (blk + 1) * 4 * WP, :].astype(F32)
            s = (s.reshape(4, WP, WP) + side[None]).reshape(4 * WP, WP)
            e = jnp.exp(s - jnp.max(s, axis=-1, keepdims=True))
            a = (e * (1.0 / jnp.sum(e, axis=-1, keepdims=True))).astype(BF)
            attn[aligned((w * 4 + blk) * 4 * WP, 4 * WP), :] = a
            attended[rows, blk * 128 : blk * 128 + 128] = pick_heads(mm(a, v), masks).astype(BF)
        return carry

    lax.fori_loop(0, tokens // WP, window, 0, unroll=3)
    keep(1)
    keep(2)
    ready(1)
    free(3)
    for j in range(2):
        cols = slice(j * 256, j * 256 + 256)
        hidden[:, cols] = x_ref[:, cols].astype(F32) + (mm(attended[...], wproj[:, cols]) + small[4:5, cols])
    keep(3)
    unit_two, _ = unit_norm(hidden[...])
    n_ref[...] = (unit_two * small[5:6] + small[6:7]).astype(BF)
    ready(2)
    free(4)
    free(5)
    for j in range(8):
        cols = slice(j * 256, j * 256 + 256)
        u = mm(n_ref[...], wfc1[:, cols]) + small[8 + j // 2 : 9 + j // 2, (j % 2) * 256 : (j % 2) * 256 + 256]
        cdf = 0.5 + 0.5 * lax.erf(u * (0.5**0.5))
        act[:, cols] = (u * cdf).astype(BF)
        dgelu[:, cols] = (cdf + u * (jnp.exp(u * u * -0.5) * ((2 * np.pi) ** -0.5))).astype(BF)
    keep(4)
    keep(5)
    ready(3)


def layer_out(bufs, weights, small, out):
    hidden, act = bufs[3], bufs[4]
    for j in range(2):
        cols = slice(j * 256, j * 256 + 256)
        out[:, cols] = (hidden[:, cols] + (mm(act[...], weights[3][:, cols]) + small[7:8, cols])).astype(BF)


def forward_kernel(xh, cot, gain_one, bias_one, query_bias, value_bias, proj_bias, gain_two, bias_two, fc2_bias, fc1_bias,
                   merge_gain, merge_bias, table, turned, masks, take, pick, send0, own1, halo1, own2, halo2, select, *refs):
    own, saved, other = refs[0:5], (refs[5:12], refs[12:19]), refs[19:23]
    merged, normed, grad_cots, merge_sums, small, grad = refs[23:29]
    weights, wm, bufs = (refs[29:33], refs[33:37]), refs[37], refs[38:44]
    x_ref, n_ref, pos, rows_in, pack_in, cots, out, halo_out, halo_in = refs[44:53]
    rows_ref, ghead, msel, mrecv = refs[53:57]
    load_sem, keep_sem, other_sem, send_sem, recv_sem = refs[57:62]
    core, me = lax.axis_index("pipe"), lax.axis_index("dp")
    partner = 1 - core
    pages = x_ref.shape[0] // (2 * WP)

    def remote(i, source, target):
        return pltpu.make_async_remote_copy(
            src_ref=source, dst_ref=target, send_sem=send_sem.at[i], recv_sem=recv_sem.at[i],
            device_id=(partner, me), device_id_type=MESH)

    shared = [(xh, rows_in), (pack_in.at[core], pack_in), (cot, cots), (own[4], wm)]
    local = [pltpu.make_async_copy(source, target.at[core], load_sem.at[4 + i]) for i, (source, target) in enumerate(shared)]
    sends = [remote(4 + i, source, target.at[core]) for i, (source, target) in enumerate(shared)]
    gets = [remote(4 + i, source, target.at[partner]) for i, (source, target) in enumerate(shared)]

    def loading(layer, i):
        return pltpu.make_async_copy(own[i], weights[layer][i], load_sem.at[i])

    def pushing(layer, i):
        return remote(i, own[i], weights[layer][i])

    def each_core(action):
        for layer in range(2):
            @pl.when(core == layer)
            def _():
                action(layer)

    local[0].start()

    def load(layer):
        for i in range(4):
            loading(layer, i).start()

    each_core(load)
    local[2].start()
    local[3].start()
    singles = [gain_one, bias_one, query_bias, value_bias, proj_bias, gain_two, bias_two, fc2_bias]
    rows = [row[...].astype(F32) for row in singles] + [fc1_bias[:, k * 512 : k * 512 + 512].astype(F32) for k in range(4)]
    pack_in[core, 0:16, :] = jnp.concatenate(rows + [jnp.zeros((4, 512), F32)], axis=0).astype(BF)
    entries = mm(table[...], turned[...]).astype(BF)
    pack_in[core, 16:32, :] = jnp.concatenate([entries, jnp.zeros((16, 128), BF)], axis=1)
    barrier = pltpu.get_barrier_semaphore()
    pl.semaphore_signal(barrier, inc=1, device_id=(partner, me), device_id_type=MESH)
    pl.semaphore_wait(barrier, 1)
    sends[1].start()
    sends[0].start()

    def push(layer):
        for i in range(4):
            pushing(layer, i).start()

    each_core(push)
    sends[2].start()
    sends[3].start()

    def ready(layer):
        def wait(i):
            @pl.when(core == layer)
            def _():
                loading(layer, i).wait()

            @pl.when(core != layer)
            def _():
                pushing(layer, i).wait_recv()
                pltpu.make_async_copy(weights[layer][i], other[i], other_sem.at[i]).start()

        return wait

    def kept(layer, i):
        source = bufs[i] if i < 6 else x_ref
        return pltpu.make_async_copy(source, saved[layer][i], keep_sem.at[layer, i])

    gets[1].wait_recv()
    small[...] = pack_in[:, 0:16, :].astype(F32)
    expand_table(pack_in.at[0, 16:32, 0:384], select, pos)
    local[0].wait()
    gets[0].wait_recv()
    for half in range(2):
        for p in range(pages):
            x_ref[p * 2 * WP : (p + 1) * 2 * WP, half * 256 : half * 256 + 256] = mm(
                take[core], rows_in[half, p * 400 : (p + 1) * 400, :]).astype(BF)
    kept(0, 6).start()
    block_forward(x_ref, small[0], weights[0], ready(0), pos, masks.at[0], bufs, n_ref,
                  lambda i: kept(0, i).start(), lambda i: None)
    layer_out(bufs, weights[0], small[0], out)
    halo_out[0] = by_page(pages, send0, out).astype(BF)
    halo = [remote(8 + i, halo_out.at[i], halo_in.at[i]) for i in range(3)]
    halo[0].start()
    expand_table(pack_in.at[1, 16:32, 0:384], select, pos)
    kept(0, 6).wait()
    x_ref[...] = by_page(pages, own1, out).astype(BF)
    halo[0].wait_recv()
    x_ref[...] = x_ref[...] + by_page(pages, halo1, halo_in[0]).astype(BF)
    kept(1, 6).start()
    block_forward(x_ref, small[1], weights[1], ready(1), pos, masks.at[1 + core], bufs, n_ref,
                  lambda i: kept(1, i).start(), lambda i: kept(0, i).wait())
    layer_out(bufs, weights[1], small[1], out)
    halo_out[1] = by_page_back(pages, halo1, out).astype(BF)
    halo[1].start()

    count = rows_ref.shape[0]
    local[2].wait()
    gets[2].wait_recv()
    for half in range(2):
        grad_cots[half] = mm(pick[core], cots[half]).astype(BF)
    for k in range(4):
        rows_ref[:, k * 512 : k * 512 + 512] = mm(own2[k * count : (k + 1) * count, :], out[...])
    halo[1].wait_recv()
    for k in range(4):
        cols = slice(k * 512, k * 512 + 512)
        rows_ref[:, cols] = rows_ref[:, cols] + mm(halo2[k * count : (k + 1) * count, :], halo_in[1])
    unit, inv_std = unit_norm(rows_ref[...])
    scale, shift = [jnp.concatenate([v[i : i + 1].astype(F32) for i in range(16)], axis=1) for v in (merge_gain[...], merge_bias[...])]
    normed[...] = (unit * scale + shift).astype(BF)
    local[3].wait()
    gets[3].wait_recv()
    for half in range(2):
        for k in range(4):
            cols = slice(k * 512, k * 512 + 512)
            term = mm_nt(grad_cots[half], wm[half, cols, :]).astype(BF).astype(F32)
            ghead[:, cols] = term if half == 0 else ghead[:, cols] + term
    grad_head = ghead[...]
    over_rows = [jnp.sum(grad_head * unit, axis=0, keepdims=True), jnp.sum(grad_head, axis=0, keepdims=True)]
    for i in range(2):
        for k in range(4):
            merge_sums[i * 4 + k : i * 4 + k + 1] = over_rows[i][:, k * 512 : k * 512 + 512]
    grad_rows = unit_norm_back(grad_head, unit, inv_std, scale).astype(BF)
    stacked = jnp.concatenate([grad_rows[:, k * 512 : k * 512 + 512] for k in range(4)], axis=0)
    halo_out[2] = mm_tn(halo2[...], stacked).astype(BF)
    halo[2].start()
    grad[...] = mm_tn(own2[...], stacked)
    for half in range(2):
        msel[half] = mm(normed[...], wm[half]).astype(BF)
    rows_copy = remote(11, msel.at[partner], mrecv)
    rows_copy.start()
    halo[2].wait_recv()
    grad[...] = grad[...] + by_page(pages, halo1, halo_in[2])
    rows_copy.wait_recv()
    merged[...] = (mm_tn(pick[core], msel[core]) + mm_tn(pick[partner], mrecv[...])).astype(BF)

    for copy in sends + halo + [rows_copy]:
        copy.wait_send()
    for i in range(7):
        kept(1, i).wait()

    def settle(layer):
        for i in range(4):
            pushing(layer, i).wait_send()
            pltpu.make_async_copy(weights[1 - layer][i], other[i], other_sem.at[i]).wait()

    each_core(settle)


class Chips:
    def __init__(self):
        me = lax.axis_index("dp")
        x, y, low, high = [lax.rem(me // stride, 2) for stride in (1, 2, 4, 8)]
        self.along_x = (me + 1 - 2 * x, x)
        self.along_y = (me + 2 - 4 * y, y)
        self.inner = lax.rem(low + high, 2)
        self.near_z = (me + 4 - 8 * low, self.inner)
        self.far_z = (me + 12 - 8 * low - 16 * high, high)


def aligned(start, count, step=16):
    return pl.ds(pl.multiple_of(start, step), count)


class Exchange:
    def __init__(self, dp, acc, paired, slots, total, sems):
        self.core, self.me = lax.axis_index("pipe"), lax.axis_index("dp")
        self.partner = 1 - self.core
        self.acc, self.paired, self.slots = acc, paired, slots
        self.total = total
        self.pair_send, self.pair_recv, self.store_sem, self.send_sem, self.recv_sem = sems
        self.chips = Chips() if dp == CHIPS else None
        self.steps = STEPS if self.chips else 0
        self.table = SCHEDULE if self.chips else FALLBACK

    def greet(self):
        barrier = pltpu.get_barrier_semaphore()
        chips = self.chips
        peers = [chip for chip, _ in (chips.along_x, chips.along_y, chips.near_z, chips.far_z)] if chips else []
        pl.semaphore_signal(barrier, inc=1, device_id=(self.partner, self.me), device_id_type=MESH)
        for chip in peers:
            pl.semaphore_signal(barrier, inc=1, device_id=(self.core, chip), device_id_type=MESH)
        pl.semaphore_wait(barrier, 1 + len(peers))

    def to_partner(self, unit, source):
        return pltpu.make_async_remote_copy(
            src_ref=source, dst_ref=self.paired.at[aligned(unit * UNIT, UNIT)],
            send_sem=self.pair_send.at[unit], recv_sem=self.pair_recv.at[unit],
            device_id=(self.partner, self.me), device_id_type=MESH)

    def ring_units(self, number):
        start, stop = EMITS[number]
        first = ROWS + number % RING * 512
        return [(start // UNIT + i, self.acc.at[first + i * UNIT : first + (i + 1) * UNIT])
                for i in range((stop - start) // UNIT)]

    def emit(self, number, owner, value):
        start, stop = EMITS[number]
        if number >= RING:
            @pl.when(jnp.logical_not(owner))
            def _():
                for unit, source in self.ring_units(number - RING):
                    self.to_partner(unit, source).wait_send()

        place = jnp.where(owner, start, ROWS + number % RING * 512)
        self.acc[aligned(place, stop - start), :] = value

        @pl.when(jnp.logical_not(owner))
        def _():
            for unit, source in self.ring_units(number):
                self.to_partner(unit, source).start()

    def kind_of(self, q):
        kind = jnp.int32(0)
        for i, k in enumerate(KINDS):
            kind = jnp.where(q == i, k, kind) if k else kind
        return kind

    def step_of(self, q, kind, step, z_last):
        chips = self.chips
        swapped = lax.rem(kind, 2)
        first = [jnp.where(swapped == 0, u, v) for u, v in zip(chips.along_x, chips.along_y)]
        second = [jnp.where(swapped == 0, u, v) for u, v in zip(chips.along_y, chips.along_x)]
        order = [first, second, chips.near_z, chips.far_z] if z_last else [chips.near_z, chips.far_z, first, second]
        lengths = [CHUNK // 2, CHUNK // 4, CHUNK // 4 if z_last else CHUNK // 8, CHUNK // 8 if z_last else CHUNK // 16]
        base = q * CHUNK
        for i in range(step):
            if not (z_last and i == 2):
                base = base + order[i][1] * lengths[i]
        chip, keep = order[step]
        length = lengths[step]
        slot = q * SLOT + sum(lengths[:step])
        if z_last and step == 2:
            return chip, base, base, length, slot, chips.inner == 0, chips.inner == 1
        when = chips.inner == 1 if z_last and step == 3 else None
        return chip, base + (1 - keep) * length, base + keep * length, length, slot, when, when

    def move(self, q, kind, e, z_last):
        half = STEPS // 2
        chip, give, keep, length, slot, sends, gets = self.step_of(q, kind, min(e, STEPS - 1 - e), z_last)
        target = aligned(slot, length)
        if e < half:
            ends = dict(src_ref=self.acc.at[aligned(give, length)], dst_ref=self.slots.at[target])
        else:
            sends, gets = gets, sends
            ends = dict(src_ref=self.paired.at[aligned(keep, length)], dst_ref=self.paired.at[aligned(keep, length)])
        copy = pltpu.make_async_remote_copy(
            send_sem=self.send_sem.at[q, e], recv_sem=self.recv_sem.at[q, e],
            device_id=(self.core, chip), device_id_type=MESH, **ends)
        return copy, sends, gets, aligned(keep, length), target

    def begin_step(self, q, kind, e, z_last):
        copy, sends, _, _, _ = self.move(q, kind, e, z_last)
        if sends is None:
            copy.start()
        else:
            pl.when(sends)(copy.start)

    def end_step(self, q, kind, e, z_last):
        copy, sends, gets, kept, target = self.move(q, kind, e, z_last)

        def got():
            copy.wait_recv()
            if e < STEPS // 2:
                into = self.acc if e < STEPS // 2 - 1 else self.paired
                into[kept, :] = (self.acc[kept, :].astype(F32) + self.slots[target, :].astype(F32)).astype(BF)

        if sends is None:
            got()
            copy.wait_send()
        else:
            pl.when(gets)(got)
            pl.when(sends)(copy.wait_send)

    def store(self, q):
        rows = aligned(q * CHUNK, CHUNK)
        return pltpu.make_async_copy(self.paired.at[rows], self.total.at[rows], self.store_sem.at[q])

    def event(self, q, e):
        if e == 0:
            into = self.acc if self.steps else self.paired

            def add(i, carry):
                unit = q * (CHUNK // UNIT) + i
                rows = aligned(unit * UNIT, UNIT)
                self.to_partner(unit, self.acc.at[rows]).wait_recv()
                into[rows, :] = (self.acc[rows, :].astype(F32) + self.paired[rows, :].astype(F32)).astype(BF)
                return carry

            lax.fori_loop(0, CHUNK // UNIT, add, 0)
        if self.steps:
            kind = self.kind_of(q)
            for z_last in (True, False):
                @pl.when(kind < 2 if z_last else kind >= 2)
                def _():
                    if e > 0:
                        self.end_step(q, kind, e - 1, z_last)
                    if e < STEPS:
                        self.begin_step(q, kind, e, z_last)

        if e == self.steps:
            self.store(q).start()

    def tick(self, t, done):
        def counts(table):
            def among(ticks, low, high):
                if low == high:
                    return jnp.int32(low)
                middle = (low + high) // 2
                return jnp.where(t >= ticks[middle], among(ticks, middle + 1, high), among(ticks, low, middle))

            return [among([chunk[e] for chunk in table], 0, len(table)) for e in range(self.steps + 1)]

        upto = lax.cond(self.core == 0, lambda: counts(self.table[0]), lambda: counts(self.table[1]))
        for e in reversed(range(self.steps + 1)):
            def one(q, carry):
                self.event(q, e)
                return carry

            lax.fori_loop(done[e], upto[e], one, 0)
        return upto

    def end(self):
        def stored(q, carry):
            self.store(q).wait()
            return carry

        lax.fori_loop(0, ROWS // CHUNK, stored, 0)

        for number in range(len(EMITS) - RING, len(EMITS)):
            for unit, source in self.ring_units(number):
                self.to_partner(unit, source).wait_send()


def backward_kernel(dp, grad_own, own1, halo1, send0, place_back, small, select, back, merge_sums, *refs):
    saved = (refs[0:7], refs[7:14])
    own, other, normed_hbm, cots_hbm = refs[14:18], refs[18:22], refs[22], refs[23]
    total, grad_x = refs[24:26]
    bufs, weights, refs = refs[26:33], refs[33:37], refs[37:]
    gm, n_ref, g_ref, work, score_sum, grad_small, halo_out, halo_in, rows_out, rows_in, page_rows, normed, cots = refs[0:13]
    acc, paired, slots, load_sem, misc_sem = refs[13:18]
    qkv, attn, attended, hidden, act, dgelu, x_ref = bufs
    wqkv, wproj, wfc1, wfc2 = weights
    gpre, dqkv = dgelu, qkv
    ex = Exchange(dp, acc, paired, slots, total, refs[18:23])
    core = ex.core
    tokens = g_ref.shape[0]
    low_masks, masks = head_masks(BF), head_masks(F32)
    def fetch(layer, names):
        for name in names:
            if name < 7:
                pltpu.make_async_copy(saved[layer][name], bufs[name], load_sem.at[layer, name]).start()
            else:
                i = name - 7

                @pl.when(core == layer)
                def _():
                    pltpu.make_async_copy(own[i], weights[i], load_sem.at[layer, name]).start()

                @pl.when(core != layer)
                def _():
                    pltpu.make_async_copy(other[i], weights[i], load_sem.at[layer, name]).start()

    def fetched(layer, *names):
        for name in names:
            target = bufs[name] if name < 7 else weights[name - 7]
            source = saved[0][name] if name < 7 else own[name - 7]
            pltpu.make_async_copy(source, target, load_sem.at[layer, name]).wait()

    def refill(step, names):
        @pl.when(step == 0)
        def _():
            fetch(0, names)

    fetch_order = [10, 5, 4, 3, 9, 2, 8, 0, 1, 7, 6]
    grad_copy = pltpu.make_async_copy(grad_own, g_ref, misc_sem.at[0])
    merge_copies = [pltpu.make_async_copy(normed_hbm, normed, misc_sem.at[6]), pltpu.make_async_copy(cots_hbm, cots, misc_sem.at[7])]
    for copy in merge_copies:
        copy.start()
    grad_copy.start()
    fetch(1, fetch_order)
    ex.greet()
    halo_copy = pltpu.make_async_remote_copy(
        src_ref=halo_out, dst_ref=halo_in, send_sem=misc_sem.at[1], recv_sem=misc_sem.at[2],
        device_id=(ex.partner, ex.me), device_id_type=MESH)
    rows_copy = pltpu.make_async_remote_copy(
        src_ref=rows_out, dst_ref=rows_in, send_sem=misc_sem.at[3], recv_sem=misc_sem.at[4],
        device_id=(ex.partner, ex.me), device_id_type=MESH)
    last_copy = pltpu.make_async_copy(page_rows, grad_x, misc_sem.at[5])
    pages = tokens // (2 * WP)

    def half_of(half):
        return pl.ds(pl.multiple_of(half * 256, 256), 256)

    def send_rows():
        rows_out[...] = g_ref[:, half_of(ex.partner)].astype(BF)
        rows_copy.start()

    def place_rows():
        rows_copy.wait()
        mine = g_ref[:, half_of(core)]
        high = mine.astype(BF)
        low = (mine - high.astype(F32)).astype(BF)
        for p in range(pages):
            rows = slice(p * 2 * WP, (p + 1) * 2 * WP)
            placed = (
                mm(place_back[core], high[rows]) + mm(place_back[core], low[rows]) + mm(place_back[ex.partner], rows_in[rows, :]))
            for r in range(PAGE):
                page_rows[p, r] = placed[r * PAGE : r * PAGE + PAGE]
        last_copy.start()


    def put(row, value):
        grad_small[row : row + 1] = jnp.sum(value, axis=0, keepdims=True)

    def fc2_piece(step, layer, half):
        vectors = small.at[layer]
        owner = core == layer
        if half == 0:
            grad_small[...] = jnp.zeros_like(grad_small)

            @pl.when(step == 0)
            def _():
                grad_copy.wait()

            @pl.when(step == 1)
            def _():
                halo_copy.wait()
                g_ref[...] = g_ref[...] + by_page_back(pages, send0, halo_in[...])

            gm[...] = g_ref[...].astype(BF)
            put(7, gm[...].astype(F32))
            fetched(layer, 10, 5)
        for j in range(half * 4, half * 4 + 4):
            cols = slice(j * 256, j * 256 + 256)
            low = (mm_nt(gm[...], wfc2[cols, :]) * dgelu[:, cols].astype(F32)).astype(BF)
            gpre[:, cols] = low
            grad_small[8 + j // 2 : 9 + j // 2, (j % 2) * 256 : (j % 2) * 256 + 256] = jnp.sum(
                low.astype(F32), axis=0, keepdims=True)
        if half == 0:
            fetched(layer, 4)
        for b in range(half * 2, half * 2 + 2):
            ex.emit(4 + b, owner, mm_tn(act[:, b * 512 : b * 512 + 512], gm[...]).astype(BF))
        if half == 1:
            refill(step, [4, 10])

    def fc1_piece(step, layer):
        fetched(layer, 3)
        unit, _ = unit_norm(hidden[...])
        n_ref[...] = (unit * small[layer, 5:6] + small[layer, 6:7]).astype(BF)
        for b in range(4):
            ex.emit(8 + b, core == layer, mm_tn(n_ref[...], gpre[:, b * 512 : b * 512 + 512]).astype(BF))

    def norm_two_piece(step, layer):
        fetched(layer, 9)
        for j in range(2):
            work[:, j * 256 : j * 256 + 256] = mm_nt(gpre[...], wfc1[j * 256 : j * 256 + 256, :])
        unit, inv_std = unit_norm(hidden[...])
        dn = work[...]
        put(5, dn * unit)
        put(6, dn)
        g_ref[...] = g_ref[...] + unit_norm_back(dn, unit, inv_std, small[layer, 5:6])
        gm[...] = g_ref[...].astype(BF)
        put(4, gm[...].astype(F32))
        refill(step, [5, 3, 9])

    def proj_piece(step, layer):
        fetched(layer, 2, 8)
        ex.emit(12, core == layer, mm_tn(attended[...], gm[...]).astype(BF))
        for j in range(2):
            n_ref[:, j * 256 : j * 256 + 256] = mm_nt(gm[...], wproj[j * 256 : j * 256 + 256, :]).astype(BF)
        score_sum[...] = jnp.zeros_like(score_sum)
        fetched(layer, 0, 1)
        refill(step, [2, 8])

    def window(w, carry):
        rows = aligned(w * WP, WP)
        for blk in range(4):
            cols = [slice(i * 512 + blk * 128, i * 512 + blk * 128 + 128) for i in range(3)]
            q, k, v = [qkv[rows, c] for c in cols]
            g = n_ref[rows, cols[0]]
            a = attn[aligned((w * 4 + blk) * 4 * WP, 4 * WP), :]
            p = mm_nt(stack_heads(g, low_masks), v)
            wide = a.astype(F32)
            ap = wide * p
            low = (ap - wide * jnp.sum(ap, axis=-1, keepdims=True)).astype(BF)
            score_sum[blk * 4 * WP : (blk + 1) * 4 * WP, :] += low.astype(F32)
            gt, qt = g.T, q.T
            dv = [mm(gt[h * 32 : h * 32 + 32], a[h * WP : (h + 1) * WP]) for h in range(4)]
            dk = [mm(qt[h * 32 : h * 32 + 32], low[h * WP : (h + 1) * WP]) * 32**-0.5 for h in range(4)]
            dqkv[rows, cols[2]] = jnp.concatenate(dv, axis=0).astype(BF).T
            dqkv[rows, cols[1]] = jnp.concatenate(dk, axis=0).astype(BF).T
            dqkv[rows, cols[0]] = (pick_heads(mm(low, k), masks) * 32**-0.5).astype(BF)
        return carry

    def attention_piece(step, layer, half):
        count = tokens // WP // 2
        lax.fori_loop(0, count, lambda i, carry: window(half * count + i, carry), 0, unroll=3)

        @pl.when(half == 1)
        def _():
            refill(step, [1])

    def qkv_piece(step, layer):
        fetched(layer, 6)
        unit, _ = unit_norm(x_ref[...].astype(F32))
        n_ref[...] = (unit * small[layer, 0:1] + small[layer, 1:2]).astype(BF)
        for b in range(3):
            ex.emit(13 + b, core == layer, mm_tn(n_ref[...], dqkv[:, b * 512 : b * 512 + 512]).astype(BF))
        put(2, dqkv[:, 0:512].astype(F32))
        put(3, dqkv[:, 1024:1536].astype(F32))

    def norm_one_piece(step, layer):
        fetched(layer, 7)
        for j in range(2):
            work[:, j * 256 : j * 256 + 256] = mm_nt(dqkv[...], wqkv[j * 256 : j * 256 + 256, :])
        unit, inv_std = unit_norm(x_ref[...].astype(F32))
        dn = work[...]
        put(0, dn * unit)
        put(1, dn)
        g_ref[...] = g_ref[...] + unit_norm_back(dn, unit, inv_std, small[layer, 0:1])

        @pl.when(step == 0)
        def _():
            gm[...] = g_ref[...].astype(BF)
            halo_out[...] = by_page_back(pages, halo1, gm[...]).astype(BF)
            halo_copy.start()
            g_ref[...] = by_page_back(pages, own1, gm[...])

        refill(step, [0, 7, 6])
        reduce_table(score_sum, select, back, grad_small.at[16:32])
        grad_small[32:40] = merge_sums[...]
        ex.emit(16, core == layer, jnp.concatenate([grad_small[...], jnp.zeros((UNIT - 48, 512), F32)], axis=0).astype(BF))

    pieces = [partial(fc2_piece, half=0), partial(fc2_piece, half=1), fc1_piece, norm_two_piece, proj_piece,
              attention_piece, None, qkv_piece, norm_one_piece]

    for copy in merge_copies:
        copy.wait()
    for half in range(2):
        for k in range(4):
            ex.emit(k, core == half, mm_tn(normed[:, k * 512 : k * 512 + 512], cots[half]).astype(BF))

    def tick(t, done):
        done = ex.tick(t, done)
        step, place = t // len(pieces), lax.rem(t, len(pieces))
        layer = 1 - step
        for i, piece in enumerate(pieces):
            if piece is attention_piece:
                @pl.when(jnp.logical_and(jnp.logical_or(place == i, place == i + 1), step < 2))
                def _():
                    attention_piece(step, layer, place - i)
            elif piece is not None:
                @pl.when(jnp.logical_and(place == i, step < 2))
                def _():
                    piece(step, layer)

        @pl.when(t == 2 * len(pieces))
        def _():
            send_rows()

        @pl.when(t == 2 * len(pieces) + 2)
        def _():
            place_rows()

        return done

    ticks = 1 + max(t for core in ex.table for chunk in core for t in chunk)
    lax.fori_loop(0, max(ticks, 2 * len(pieces) + 3), tick, [jnp.int32(0)] * (ex.steps + 1))
    ex.end()
    last_copy.wait()


def widen_kernel(total, page_rows, turn, wqkv, wproj, wfc1, wfc2, wmerge, pages_out, *refs):
    singles, (fc1_bias, merge_gain, merge_bias, table, rows, stage, passing, load_sem, store_sem, pass_sem) = refs[0:8], refs[8:]
    pass_in = pltpu.make_async_copy(page_rows, passing, pass_sem.at[0])
    pass_out = pltpu.make_async_copy(passing, pages_out, pass_sem.at[1])
    pass_in.start()
    blocks = [(b * 512, wmerge.at[b * 512 : b * 512 + 512, :]) for b in range(4)]
    blocks += [(2048 + b * 512, wfc2.at[b * 512 : b * 512 + 512, :]) for b in range(4)]
    blocks += [(4096 + b * 512, wfc1.at[:, b * 512 : b * 512 + 512]) for b in range(4)]
    blocks += [(6144, wproj)]
    blocks += [(6656 + b * 512, wqkv.at[:, b * 512 : b * 512 + 512]) for b in range(3)]
    loads = []
    for i, (start, _) in enumerate(blocks + [(8192, None)]):
        count = min(512, total.shape[0] - start)
        copy = pltpu.make_async_copy(total.at[start : start + count], rows.at[start : start + count], load_sem.at[i])
        copy.start()
        loads.append(copy)
    stores = []
    for i, (start, target) in enumerate(blocks):
        slot = i % 4
        loads[i].wait()
        if i == 1:
            pass_in.wait()
            pass_out.start()
        if i >= 4:
            stores[i - 4].wait()
        stage[slot] = rows[start : start + 512, :].astype(F32)
        copy = pltpu.make_async_copy(stage.at[slot], target, store_sem.at[slot])
        copy.start()
        stores.append(copy)
    loads[-1].wait()
    tail = rows[8192:8240, :].astype(F32)
    for k in range(8):
        singles[k][...] = tail[k : k + 1]
    for k in range(4):
        cols = slice(k * 512, k * 512 + 512)
        fc1_bias[:, cols] = tail[8 + k : 9 + k]
        merge_gain[:, cols] = tail[32 + k : 33 + k]
        merge_bias[:, cols] = tail[36 + k : 37 + k]
    high = rows[8208:8224, 0:384].astype(BF)
    table[...] = mm(high, turn[...])
    for copy in stores[-4:]:
        copy.wait()
    pass_out.wait()


HBM = pl.BlockSpec(memory_space=pl.ANY)
VMEM = pl.BlockSpec(memory_space=pltpu.VMEM)


def scratch_of(entry):
    if entry is None:
        return pltpu.SemaphoreType.DMA
    if isinstance(entry, int):
        return pltpu.SemaphoreType.DMA((entry,))
    if isinstance(entry[0], int):
        return pltpu.SemaphoreType.DMA(entry)
    return pltpu.VMEM(*entry)


def call(kernel, args, outs, scratch, name, collective_id=None):
    return pl.pallas_call(
        kernel,
        out_shape=[jax.ShapeDtypeStruct(s, d) for s, d, _ in outs],
        in_specs=[spec for _, spec in args],
        out_specs=[spec for _, _, spec in outs],
        scratch_shapes=[scratch_of(s) for s in scratch],
        compiler_params=pltpu.CompilerParams(
            vmem_limit_bytes=VMEM_LIMIT, collective_id=collective_id, has_side_effects=collective_id is not None),
        name=name,
    )(*[value for value, _ in args])


def shards(
    page_inputs, gain_one, bias_one, qkv_weight, query_bias, value_bias, bias_table, proj_weight, proj_bias,
    gain_two, bias_two, fc1_weight, fc1_bias, fc2_weight, fc2_bias, merge_gain, merge_bias, merge_weight, cotangent,
):
    dp = lax.axis_size("dp")
    pages = page_inputs.shape[0]
    tokens = pages * 2 * WP
    heads = bias_table.shape[2]
    table = bias_table.shape[1]
    place = place_tables(pages)
    select, back = code_matrices()
    merged_rows, cot_rows = place["pick"].shape[1:]

    turned = np.zeros((table, 384), np.float32)
    for u in range(table):
        turned[table - 1 - u, (u - 4) % 384] = 1
    params = [gain_one, bias_one, query_bias, value_bias, proj_bias, gain_two, bias_two, fc2_bias, fc1_bias,
              merge_gain.reshape(16, 128), merge_bias.reshape(16, 128), bias_table[0].T, jnp.asarray(turned, BF)]
    own = [qkv_weight[0], proj_weight[0], fc1_weight[0], fc2_weight[0]]
    xh = page_inputs.reshape(pages * 400, 256)
    cot = cotangent.transpose(1, 2, 0, 3)
    cot = jnp.pad(cot, ((0, 0), (0, 0), (0, cot_rows // AREA - pages), (0, 0))).reshape(cot_rows, 512)

    def at(spec, *values):
        return [(v, spec) for v in values]

    rows = ((tokens, 512), BF)
    wide_rows = ((tokens, 512), F32)
    saved_shapes = [((tokens, 1536), BF), ((pages * 2 * heads * WP, WP), BF), rows, wide_rows,
                    ((tokens, 2048), BF), ((tokens, 2048), BF)]
    weight_shapes = [(w.shape, BF) for w in own]
    halo = ((pages * WP, 512), BF)
    halos = ((3, pages * WP, 512), BF)
    parts_shape = ((2, 2048, 512), BF)
    mrows = (merged_rows, 512)
    results = call(
        forward_kernel,
        at(HBM, xh, cot) + at(VMEM, *params, window_masks(),
                                    *[place[n] for n in ("take", "pick", "send0", "own1", "halo1", "own2", "halo2")], select)
        + at(HBM, *own, merge_weight),
        [(*shape, HBM) for shape in (saved_shapes + [rows]) * 2 + weight_shapes]
        + [((cot_rows, 512), BF, VMEM), ((merged_rows, 2048), BF, VMEM), ((2, *mrows), BF, VMEM), ((8, 512), F32, VMEM), ((2, 16, 512), F32, VMEM), (*wide_rows, VMEM)],
        weight_shapes * 2 + [parts_shape] + saved_shapes
        + [rows, rows, ((heads * WP, WP), BF), ((2, *xh.shape), BF), ((2, 32, 512), BF), ((2, cot_rows, 512), BF), rows, halos, halos,
           ((merged_rows, 2048), F32), ((merged_rows, 2048), F32), ((2, *mrows), BF), (mrows, BF),
           8, (2, 7), 4, 12, 12],
        "forward", collective_id=1)
    saved0, saved1, other = results[0:7], results[7:14], results[14:18]
    merged, normed, cots, merge_sums, small, grad_own = results[18:]

    chunks, units = ROWS // CHUNK, ROWS // UNIT
    page_half = ((pages, PAGE, PAGE, 256), F32)
    total, grad_pages = call(
        partial(backward_kernel, dp),
        at(HBM, grad_own) + at(VMEM, place["own1"], place["halo1"], place["send0"], place["back"], small, select, back, merge_sums)
        + at(HBM, *saved0, *saved1, *own, *other, normed, cots),
        [((ROWS, 512), BF, HBM), (*page_half, HBM)],
        saved_shapes + [rows] + weight_shapes
        + [rows, rows, wide_rows, wide_rows, ((heads * WP, WP), F32), ((48, 512), F32), halo, halo,
           ((tokens, 256), BF), ((tokens, 256), BF), page_half, ((merged_rows, 2048), BF), ((2, *mrows), BF)]
        + [((ROWS + RING * 512, 512), BF), ((ROWS, 512), BF), ((chunks * SLOT, 512), BF), (2, 11), 8,
           units, units, chunks, (chunks, STEPS), (chunks, STEPS)],
        "backward", collective_id=0)
    if dp != CHIPS:
        total = lax.psum(total.astype(F32), "dp")

    turn = np.zeros((384, table), np.float32)
    for u in range(table):
        turn[u + 3, table - 1 - u] = 1
    wide_row = ((1, 2048), F32, VMEM)
    g_qkv, g_proj, g_fc1, g_fc2, g_merge, grad_pages, *single, g_fc1_bias, g_gain, g_bias, g_table = call(
        widen_kernel, at(HBM, total, grad_pages) + at(VMEM, jnp.asarray(turn, BF)),
        [((512, 1536), F32, HBM), ((512, 512), F32, HBM), ((512, 2048), F32, HBM), ((2048, 512), F32, HBM),
         ((2048, 512), F32, HBM), (*page_half, HBM)] + [((1, 512), F32, VMEM)] * 8
        + [wide_row, wide_row, wide_row, ((heads, table), F32, VMEM)],
        [((ROWS, 512), total.dtype), ((4, 512, 512), F32), page_half, 17, 4, 2], "widen")
    merged = merged.reshape(10, 10, cot_rows // AREA, 512)[:, :, :pages].transpose(2, 0, 1, 3)
    return (
        merged, grad_pages,
        single[0], single[1], g_qkv[None], single[2], single[3], g_table.T[None], g_proj[None], single[4], single[5], single[6],
        g_fc1[None], g_fc1_bias, g_fc2[None], single[7], g_gain.reshape(2048), g_bias.reshape(2048), g_merge,
    )


def solution(mesh):
    row, mat = P("pipe", None), P("pipe", None, None)
    wide = P("dp", None, None, "pipe")
    in_specs = (wide, row, row, mat, row, row, mat, mat, row, row, row, mat, row, mat, row, P(), P(), P(None, "pipe"), wide)
    out_specs = (wide, wide, row, row, mat, row, row, mat, mat, row, row, row, mat, row, mat, row, P(), P(), P(None, "pipe"))
    return jax.shard_map(shards, mesh=mesh, in_specs=in_specs, out_specs=out_specs, check_vma=False)
```

```python
from functools import partial

import jax
import jax.numpy as jnp
import numpy as np
from jax import lax
from jax.experimental import pallas as pl
from jax.experimental.pallas import tpu as pltpu
from jax.sharding import PartitionSpec as P

BF = jnp.bfloat16
F32 = jnp.float32
WINDOW = 10
AREA = 100
PAGE = 20
WP = 112
EPS = 1e-05
NEG = -1e30
MESH = pl.DeviceIdType.MESH
CHIPS = 16
STEPS = 8
UNIT = 256
CHUNK = 768
ROWS = 8448
SLOT = CHUNK + CHUNK // 8
RING = 4
VMEM_LIMIT = 62 * 1024 * 1024
EMITS = [(r, r + 512) for r in range(0, 8192, 512)] + [(8192, 8448)]
KINDS = (0, 2, 0, 1, 1, 3, 1, 0, 0, 1, 2)
SCHEDULE = (
    ((1, 3, 6, 8, 9, 10, 12, 15, 17), (1, 3, 6, 8, 9, 10, 12, 15, 17), (14, 16, 18, 21, 23, 30, 36, 46, 52), (14, 16, 18, 22, 28, 32, 38, 46, 52), (15, 17, 19, 25, 31, 35, 44, 49, 54), (16, 21, 27, 34, 37, 41, 48, 51, 56), (16, 21, 27, 34, 37, 42, 48, 53, 57), (16, 21, 27, 34, 39, 45, 48, 53, 57), (20, 26, 33, 38, 43, 47, 50, 55, 58), (20, 26, 33, 38, 44, 47, 51, 55, 58), (24, 29, 36, 38, 44, 47, 51, 55, 58)),
    ((2, 4, 6, 7, 8, 9, 10, 12, 16), (2, 4, 6, 7, 8, 9, 10, 12, 16), (2, 5, 7, 9, 10, 13, 16, 18, 23), (2, 5, 7, 9, 10, 13, 16, 18, 23), (3, 6, 8, 9, 10, 13, 17, 18, 25), (4, 6, 8, 9, 10, 13, 17, 20, 28), (4, 7, 9, 10, 14, 16, 18, 24, 31), (4, 7, 9, 11, 14, 16, 19, 29, 31), (9, 11, 14, 17, 18, 21, 30, 34, 38), (9, 11, 14, 18, 22, 27, 33, 36, 39), (10, 13, 17, 18, 26, 32, 35, 37, 40)),
)
FALLBACK = (((19,),) * 11, ((19,),) * 11)


def mm(a, b):
    return lax.dot_general(a, b, (((1,), (0,)), ((), ())), preferred_element_type=F32)


def mm_nt(a, b):
    return lax.dot_general(a, b, (((1,), (1,)), ((), ())), preferred_element_type=F32)


def mm_tn(a, b):
    return lax.dot_general(a, b, (((0,), (0,)), ((), ())), preferred_element_type=F32)


def unit_norm(values):
    centred = values - jnp.mean(values, axis=-1, keepdims=True)
    inv_std = lax.rsqrt(jnp.mean(centred * centred, axis=-1, keepdims=True) + EPS)
    return centred * inv_std, inv_std


def unit_norm_back(grad_normed, unit_rows, inv_std, gain):
    grad_unit = grad_normed * gain
    return inv_std * (
        grad_unit
        - jnp.mean(grad_unit, axis=-1, keepdims=True)
        - unit_rows * jnp.mean(grad_unit * unit_rows, axis=-1, keepdims=True)
    )


def place_tables(pages):
    merged = -(-pages * 50 // 16) * 16
    group = -(-pages // 4) * 4
    cots = AREA * group
    take = np.zeros((2, 2 * WP, 400), np.float32)
    pick = np.zeros((2, merged, cots), np.float32)
    send0 = np.zeros((WP, 2 * WP), np.float32)
    own1 = np.zeros((2 * WP, 2 * WP), np.float32)
    halo1 = np.zeros((2 * WP, WP), np.float32)
    own2 = np.zeros((4 * merged, pages * 2 * WP), np.float32)
    halo2 = np.zeros((4 * merged, pages * WP), np.float32)

    def row0(r, col):
        return col // WINDOW * WP + r * WINDOW + col % WINDOW

    def row1(r, col):
        return row0(r, (col - 5) % PAGE)

    for col in range(PAGE):
        for r in range(10):
            for core in range(2):
                take[core, row0(r, col), (core * 10 + r) * PAGE + col] = 1
        for r in range(5):
            send0[r * PAGE + col, row0(r, col)] = 1
            own1[row1(r, col), row0(r + 5, col)] = 1
            halo1[row1(r + 5, col), r * PAGE + col] = 1
    for p in range(pages):
        for m in range(5):
            for n in range(10):
                for core in range(2):
                    pick[core, p * 50 + m * 10 + n, ((core * 5 + m) * 10 + n) * group + p] = 1
                for k in range(4):
                    row = k * merged + p * 50 + m * 10 + n
                    r, col = 2 * m + k % 2, 2 * n + k // 2
                    if r >= 5:
                        own2[row, p * 2 * WP + row1(r - 5, col)] = 1
                    else:
                        halo2[row, p * WP + r * PAGE + col] = 1
    return {name: jnp.asarray(t, BF) for name, t in dict(
        take=take, back=take.transpose(0, 2, 1), pick=pick, send0=send0, own1=own1, halo1=halo1, own2=own2, halo2=halo2,
        own2_back=own2.T, halo2_back=halo2.T).items()}


def window_masks():
    place = np.arange(WP)
    pad = np.where(place < AREA, 0.0, NEG)
    masks = np.zeros((3, 2, WP, WP), np.float32)
    for kind in range(3):
        for side in range(2):
            late = (place // WINDOW >= 5) * 2 * (kind == 2) + (place % WINDOW >= 5) * (side == 1) * (kind > 0)
            masks[kind, side] = np.where(late[:, None] != late[None, :], -100.0, 0.0) + pad[None, :]
    return jnp.asarray(masks)


def by_page(pages, matrix, rows):
    count = matrix.shape[1]
    return jnp.concatenate([mm(matrix[...], rows[p * count : (p + 1) * count]) for p in range(pages)], axis=0)


def by_page_back(pages, matrix, rows):
    count = matrix.shape[0]
    return jnp.concatenate([mm_tn(matrix[...], rows[p * count : (p + 1) * count]) for p in range(pages)], axis=0)


def code_matrices():
    select = np.zeros((WP, 384), np.float32)
    back = np.zeros((184, WP), np.float32)
    for i in range(AREA):
        code = (i // WINDOW) * 19 + i % WINDOW
        select[i, code] = 1
        back[183 - code, i] = 1
    return jnp.asarray(select, BF), jnp.asarray(back, BF)


def expand_table(table, select, pos):
    entries = table[...].astype(F32)
    for h in range(table.shape[0]):
        spread = pltpu.roll(jnp.broadcast_to(entries[h : h + 1, :], (184, 384)), 208, 1, stride=1, stride_axis=0)
        rows = mm(select[:, 0:184], spread.astype(BF)).astype(BF)
        pos[h * WP : (h + 1) * WP, :] = mm_nt(rows, select[...]).astype(BF)


def reduce_table(score, select, back, out):
    for h in range(out.shape[0]):
        block = score[h * WP : (h + 1) * WP, :].astype(BF)
        codes = mm(back[...], mm(block, select[:, 0:256]).astype(BF))
        codes = jnp.concatenate([codes, jnp.zeros((184, 128), F32)], axis=1)
        turned = pltpu.roll(codes, 0, 1, stride=1, stride_axis=0)
        out[h : h + 1, 0:384] = jnp.sum(turned, axis=0, keepdims=True)


def head_masks(kind):
    lane = lax.broadcasted_iota(jnp.int32, (1, 128), 1) // 32
    return [jnp.where(lane == h, 1.0, 0.0).astype(kind) for h in range(4)]


def stack_heads(block, masks):
    return jnp.concatenate([block * mask for mask in masks], axis=0)


def pick_heads(stacked, masks):
    total = stacked[0:WP] * masks[0]
    for h in range(1, 4):
        total = total + stacked[h * WP : (h + 1) * WP] * masks[h]
    return total


def block_forward(x_ref, small, weights, ready, pos, mask, bufs, n_ref, keep, free):
    qkv, attn, attended, hidden, act, dgelu = bufs
    wqkv, wproj, wfc1, _ = weights
    tokens = x_ref.shape[0]
    unit_one, _ = unit_norm(x_ref[...].astype(F32))
    n_ref[...] = (unit_one * small[0:1] + small[1:2]).astype(BF)
    zero = jnp.zeros((1, 512), F32)
    bias = [small[2:3], zero, small[3:4]]
    ready(0)
    free(0)
    for j in range(6):
        shift = bias[j // 2][:, (j % 2) * 256 : (j % 2) * 256 + 256]
        qkv[:, j * 256 : j * 256 + 256] = (mm(n_ref[...], wqkv[:, j * 256 : j * 256 + 256]) + shift).astype(BF)
    keep(0)
    free(1)
    free(2)
    low_masks, masks = head_masks(BF), head_masks(F32)

    def window(w, carry):
        rows = aligned(w * WP, WP)
        side = mask[w % 2]
        for blk in range(4):
            q, k, v = [qkv[rows, i * 512 + blk * 128 : i * 512 + blk * 128 + 128] for i in range(3)]
            s = mm_nt(stack_heads(q, low_masks), k) * 32**-0.5
            s = s + pos[blk * 4 * WP : (blk + 1) * 4 * WP, :].astype(F32)
            s = (s.reshape(4, WP, WP) + side[None]).reshape(4 * WP, WP)
            e = jnp.exp(s - jnp.max(s, axis=-1, keepdims=True))
            a = (e * (1.0 / jnp.sum(e, axis=-1, keepdims=True))).astype(BF)
            attn[aligned((w * 4 + blk) * 4 * WP, 4 * WP), :] = a
            attended[rows, blk * 128 : blk * 128 + 128] = pick_heads(mm(a, v), masks).astype(BF)
        return carry

    lax.fori_loop(0, tokens // WP, window, 0, unroll=3)
    keep(1)
    keep(2)
    ready(1)
    free(3)
    for j in range(2):
        cols = slice(j * 256, j * 256 + 256)
        hidden[:, cols] = x_ref[:, cols].astype(F32) + (mm(attended[...], wproj[:, cols]) + small[4:5, cols])
    keep(3)
    unit_two, _ = unit_norm(hidden[...])
    n_ref[...] = (unit_two * small[5:6] + small[6:7]).astype(BF)
    ready(2)
    free(4)
    free(5)
    for j in range(8):
        cols = slice(j * 256, j * 256 + 256)
        u = mm(n_ref[...], wfc1[:, cols]) + small[8 + j // 2 : 9 + j // 2, (j % 2) * 256 : (j % 2) * 256 + 256]
        cdf = 0.5 + 0.5 * lax.erf(u * (0.5**0.5))
        act[:, cols] = (u * cdf).astype(BF)
        dgelu[:, cols] = (cdf + u * (jnp.exp(u * u * -0.5) * ((2 * np.pi) ** -0.5))).astype(BF)
    keep(4)
    keep(5)
    ready(3)


def layer_out(bufs, weights, small, out):
    hidden, act = bufs[3], bufs[4]
    for j in range(2):
        cols = slice(j * 256, j * 256 + 256)
        out[:, cols] = (hidden[:, cols] + (mm(act[...], weights[3][:, cols]) + small[7:8, cols])).astype(BF)


def forward_kernel(page_places, cot_places, gain_one, bias_one, query_bias, value_bias, proj_bias, gain_two, bias_two, fc2_bias, fc1_bias,
                   merge_gain, merge_bias, table, turned, masks, take, pick, send0, own1, halo1, own2, halo2, select, own2_turned, halo2_turned, *refs):
    own, saved, other = refs[0:5], (refs[5:12], refs[12:19]), refs[19:23]
    merged, normed_out, cots_out, merge_sums, small, grad = refs[23:29]
    weights, wm, bufs = (refs[29:33], refs[33:37]), refs[37], refs[38:44]
    x_ref, n_ref, pos, rows_in, pack_in, cots, out, halo_out, halo_in = refs[44:53]
    rows_ref, ghead, msel, mrecv, cot_wide, page_wide, normed, grad_cots, own2_back, halo2_back = refs[53:63]
    load_sem, keep_sem, other_sem, send_sem, recv_sem, misc_sem = refs[63:69]
    core, me = lax.axis_index("pipe"), lax.axis_index("dp")
    partner = 1 - core
    pages = x_ref.shape[0] // (2 * WP)

    def remote(i, source, target):
        return pltpu.make_async_remote_copy(
            src_ref=source, dst_ref=target, send_sem=send_sem.at[i], recv_sem=recv_sem.at[i],
            device_id=(partner, me), device_id_type=MESH)

    shared = [(rows_in.at[core], rows_in), (pack_in.at[core], pack_in), (cots.at[core], cots), (own[4], wm)]
    local = [pltpu.make_async_copy(source, target.at[core], load_sem.at[4 + i]) for i, (source, target) in enumerate(shared)]
    sends = [remote(4 + i, source, target.at[core]) for i, (source, target) in enumerate(shared)]
    gets = [remote(4 + i, source, target.at[partner]) for i, (source, target) in enumerate(shared)]

    def loading(layer, i):
        return pltpu.make_async_copy(own[i], weights[layer][i], load_sem.at[i])

    def pushing(layer, i):
        return remote(i, own[i], weights[layer][i])

    def each_core(action):
        for layer in range(2):
            @pl.when(core == layer)
            def _():
                action(layer)


    def load(layer):
        for i in range(4):
            loading(layer, i).start()

    each_core(load)
    local[3].start()
    late = [pltpu.make_async_copy(own2_turned, own2_back, misc_sem.at[0]), pltpu.make_async_copy(halo2_turned, halo2_back, misc_sem.at[1])]
    for copy in late:
        copy.start()
    early = [pltpu.make_async_copy(normed, normed_out, misc_sem.at[2]), pltpu.make_async_copy(grad_cots, cots_out, misc_sem.at[3])]
    for p in range(pages):
        for r in range(PAGE):
            row = (p * PAGE + r) * PAGE
            page_wide[row : row + PAGE, :] = page_places[p, r].astype(F32)
    rows_in[core] = page_wide[...].astype(BF)
    singles = [gain_one, bias_one, query_bias, value_bias, proj_bias, gain_two, bias_two, fc2_bias]
    rows = [row[...].astype(F32) for row in singles] + [fc1_bias[:, k * 512 : k * 512 + 512].astype(F32) for k in range(4)]
    pack_in[core, 0:16, :] = jnp.concatenate(rows + [jnp.zeros((4, 512), F32)], axis=0).astype(BF)
    entries = mm(table[...], turned[...]).astype(BF)
    pack_in[core, 16:32, :] = jnp.concatenate([entries, jnp.zeros((16, 128), BF)], axis=1)
    barrier = pltpu.get_barrier_semaphore()
    pl.semaphore_signal(barrier, inc=1, device_id=(partner, me), device_id_type=MESH)
    pl.semaphore_wait(barrier, 1)
    sends[1].start()
    sends[0].start()

    def push(layer):
        for i in range(4):
            pushing(layer, i).start()

    each_core(push)
    cot_wide[...] = jnp.zeros_like(cot_wide)
    group = cot_wide.shape[0] // AREA
    for place in range(AREA):
        cot_wide[place * group : place * group + pages, :] = cot_places[place // 10, place % 10].astype(F32)
    cots[core] = cot_wide[...].astype(BF)
    sends[2].start()
    sends[3].start()

    def ready(layer):
        def wait(i):
            @pl.when(core == layer)
            def _():
                loading(layer, i).wait()

            @pl.when(core != layer)
            def _():
                pushing(layer, i).wait_recv()
                pltpu.make_async_copy(weights[layer][i], other[i], other_sem.at[i]).start()

        return wait

    def kept(layer, i):
        source = bufs[i] if i < 6 else x_ref
        return pltpu.make_async_copy(source, saved[layer][i], keep_sem.at[layer, i])

    gets[1].wait_recv()
    small[...] = pack_in[:, 0:16, :].astype(F32)
    expand_table(pack_in.at[0, 16:32, 0:384], select, pos)
    gets[0].wait_recv()
    for half in range(2):
        for p in range(pages):
            x_ref[p * 2 * WP : (p + 1) * 2 * WP, half * 256 : half * 256 + 256] = mm(
                take[core], rows_in[half, p * 400 : (p + 1) * 400, :]).astype(BF)
    kept(0, 6).start()
    block_forward(x_ref, small[0], weights[0], ready(0), pos, masks.at[0], bufs, n_ref,
                  lambda i: kept(0, i).start(), lambda i: None)
    layer_out(bufs, weights[0], small[0], out)
    halo_out[0] = by_page(pages, send0, out).astype(BF)
    halo = [remote(8 + i, halo_out.at[i], halo_in.at[i]) for i in range(3)]
    halo[0].start()
    expand_table(pack_in.at[1, 16:32, 0:384], select, pos)
    kept(0, 6).wait()
    x_ref[...] = by_page(pages, own1, out).astype(BF)
    halo[0].wait_recv()
    x_ref[...] = x_ref[...] + by_page(pages, halo1, halo_in[0]).astype(BF)
    kept(1, 6).start()
    block_forward(x_ref, small[1], weights[1], ready(1), pos, masks.at[1 + core], bufs, n_ref,
                  lambda i: kept(1, i).start(), lambda i: kept(0, i).wait())
    layer_out(bufs, weights[1], small[1], out)
    halo_out[1] = by_page_back(pages, halo1, out).astype(BF)
    halo[1].start()

    count = rows_ref.shape[0]
    gets[2].wait_recv()
    for half in range(2):
        grad_cots[half] = mm(pick[core], cots[half]).astype(BF)
    for k in range(4):
        rows_ref[:, k * 512 : k * 512 + 512] = mm(own2[k * count : (k + 1) * count, :], out[...])
    halo[1].wait_recv()
    for k in range(4):
        cols = slice(k * 512, k * 512 + 512)
        rows_ref[:, cols] = rows_ref[:, cols] + mm(halo2[k * count : (k + 1) * count, :], halo_in[1])
    unit, inv_std = unit_norm(rows_ref[...])
    scale, shift = [jnp.concatenate([v[i : i + 1].astype(F32) for i in range(16)], axis=1) for v in (merge_gain[...], merge_bias[...])]
    normed[...] = (unit * scale + shift).astype(BF)
    for copy in early:
        copy.start()
    local[3].wait()
    gets[3].wait_recv()
    for half in range(2):
        for k in range(4):
            cols = slice(k * 512, k * 512 + 512)
            term = mm_nt(grad_cots[half], wm[half, cols, :]).astype(BF).astype(F32)
            ghead[:, cols] = term if half == 0 else ghead[:, cols] + term
    grad_head = ghead[...]
    over_rows = [jnp.sum(grad_head * unit, axis=0, keepdims=True), jnp.sum(grad_head, axis=0, keepdims=True)]
    for i in range(2):
        for k in range(4):
            merge_sums[i * 4 + k : i * 4 + k + 1] = over_rows[i][:, k * 512 : k * 512 + 512]
    grad_rows = unit_norm_back(grad_head, unit, inv_std, scale).astype(BF)
    stacked = jnp.concatenate([grad_rows[:, k * 512 : k * 512 + 512] for k in range(4)], axis=0)
    for copy in late:
        copy.wait()
    halo_out[2] = mm(halo2_back[...], stacked).astype(BF)
    halo[2].start()
    grad[...] = mm(own2_back[...], stacked)
    for half in range(2):
        msel[half] = mm(normed[...], wm[half]).astype(BF)
    rows_copy = remote(11, msel.at[partner], mrecv)
    rows_copy.start()
    halo[2].wait_recv()
    grad[...] = grad[...] + by_page(pages, halo1, halo_in[2])
    rows_copy.wait_recv()
    merged[...] = (mm_tn(pick[core], msel[core]) + mm_tn(pick[partner], mrecv[...])).astype(BF)

    for copy in sends + halo + [rows_copy]:
        copy.wait_send()
    for copy in early:
        copy.wait()
    for i in range(7):
        kept(1, i).wait()

    def settle(layer):
        for i in range(4):
            pushing(layer, i).wait_send()
            pltpu.make_async_copy(weights[1 - layer][i], other[i], other_sem.at[i]).wait()

    each_core(settle)


class Chips:
    def __init__(self):
        me = lax.axis_index("dp")
        x, y, low, high = [lax.rem(me // stride, 2) for stride in (1, 2, 4, 8)]
        self.along_x = (me + 1 - 2 * x, x)
        self.along_y = (me + 2 - 4 * y, y)
        self.inner = lax.rem(low + high, 2)
        self.near_z = (me + 4 - 8 * low, self.inner)
        self.far_z = (me + 12 - 8 * low - 16 * high, high)


def aligned(start, count, step=16):
    return pl.ds(pl.multiple_of(start, step), count)


class Exchange:
    def __init__(self, dp, acc, paired, slots, total, sems):
        self.core, self.me = lax.axis_index("pipe"), lax.axis_index("dp")
        self.partner = 1 - self.core
        self.acc, self.paired, self.slots = acc, paired, slots
        self.total = total
        self.pair_send, self.pair_recv, self.store_sem, self.send_sem, self.recv_sem = sems
        self.chips = Chips() if dp == CHIPS else None
        self.steps = STEPS if self.chips else 0
        self.table = SCHEDULE if self.chips else FALLBACK

    def greet(self):
        barrier = pltpu.get_barrier_semaphore()
        chips = self.chips
        peers = [chip for chip, _ in (chips.along_x, chips.along_y, chips.near_z, chips.far_z)] if chips else []
        pl.semaphore_signal(barrier, inc=1, device_id=(self.partner, self.me), device_id_type=MESH)
        for chip in peers:
            pl.semaphore_signal(barrier, inc=1, device_id=(self.core, chip), device_id_type=MESH)
        pl.semaphore_wait(barrier, 1 + len(peers))

    def to_partner(self, unit, source):
        return pltpu.make_async_remote_copy(
            src_ref=source, dst_ref=self.paired.at[aligned(unit * UNIT, UNIT)],
            send_sem=self.pair_send.at[unit], recv_sem=self.pair_recv.at[unit],
            device_id=(self.partner, self.me), device_id_type=MESH)

    def ring_units(self, number):
        start, stop = EMITS[number]
        first = ROWS + number % RING * 512
        return [(start // UNIT + i, self.acc.at[first + i * UNIT : first + (i + 1) * UNIT])
                for i in range((stop - start) // UNIT)]

    def emit(self, number, owner, value):
        start, stop = EMITS[number]
        if number >= RING:
            @pl.when(jnp.logical_not(owner))
            def _():
                for unit, source in self.ring_units(number - RING):
                    self.to_partner(unit, source).wait_send()

        place = jnp.where(owner, start, ROWS + number % RING * 512)
        self.acc[aligned(place, stop - start), :] = value

        @pl.when(jnp.logical_not(owner))
        def _():
            for unit, source in self.ring_units(number):
                self.to_partner(unit, source).start()

    def kind_of(self, q):
        kind = jnp.int32(0)
        for i, k in enumerate(KINDS):
            kind = jnp.where(q == i, k, kind) if k else kind
        return kind

    def step_of(self, q, kind, step, z_last):
        chips = self.chips
        swapped = lax.rem(kind, 2)
        first = [jnp.where(swapped == 0, u, v) for u, v in zip(chips.along_x, chips.along_y)]
        second = [jnp.where(swapped == 0, u, v) for u, v in zip(chips.along_y, chips.along_x)]
        order = [first, second, chips.near_z, chips.far_z] if z_last else [chips.near_z, chips.far_z, first, second]
        lengths = [CHUNK // 2, CHUNK // 4, CHUNK // 4 if z_last else CHUNK // 8, CHUNK // 8 if z_last else CHUNK // 16]
        base = q * CHUNK
        for i in range(step):
            if not (z_last and i == 2):
                base = base + order[i][1] * lengths[i]
        chip, keep = order[step]
        length = lengths[step]
        slot = q * SLOT + sum(lengths[:step])
        if z_last and step == 2:
            return chip, base, base, length, slot, chips.inner == 0, chips.inner == 1
        when = chips.inner == 1 if z_last and step == 3 else None
        return chip, base + (1 - keep) * length, base + keep * length, length, slot, when, when

    def move(self, q, kind, e, z_last):
        half = STEPS // 2
        chip, give, keep, length, slot, sends, gets = self.step_of(q, kind, min(e, STEPS - 1 - e), z_last)
        target = aligned(slot, length)
        if e < half:
            ends = dict(src_ref=self.acc.at[aligned(give, length)], dst_ref=self.slots.at[target])
        else:
            sends, gets = gets, sends
            ends = dict(src_ref=self.paired.at[aligned(keep, length)], dst_ref=self.paired.at[aligned(keep, length)])
        copy = pltpu.make_async_remote_copy(
            send_sem=self.send_sem.at[q, e], recv_sem=self.recv_sem.at[q, e],
            device_id=(self.core, chip), device_id_type=MESH, **ends)
        return copy, sends, gets, aligned(keep, length), target

    def begin_step(self, q, kind, e, z_last):
        copy, sends, _, _, _ = self.move(q, kind, e, z_last)
        if sends is None:
            copy.start()
        else:
            pl.when(sends)(copy.start)

    def end_step(self, q, kind, e, z_last):
        copy, sends, gets, kept, target = self.move(q, kind, e, z_last)

        def got():
            copy.wait_recv()
            if e < STEPS // 2:
                into = self.acc if e < STEPS // 2 - 1 else self.paired
                into[kept, :] = (self.acc[kept, :].astype(F32) + self.slots[target, :].astype(F32)).astype(BF)

        if sends is None:
            got()
            copy.wait_send()
        else:
            pl.when(gets)(got)
            pl.when(sends)(copy.wait_send)

    def store(self, q):
        rows = aligned(q * CHUNK, CHUNK)
        return pltpu.make_async_copy(self.paired.at[rows], self.total.at[rows], self.store_sem.at[q])

    def event(self, q, e):
        if e == 0:
            into = self.acc if self.steps else self.paired

            def add(i, carry):
                unit = q * (CHUNK // UNIT) + i
                rows = aligned(unit * UNIT, UNIT)
                self.to_partner(unit, self.acc.at[rows]).wait_recv()
                into[rows, :] = (self.acc[rows, :].astype(F32) + self.paired[rows, :].astype(F32)).astype(BF)
                return carry

            lax.fori_loop(0, CHUNK // UNIT, add, 0)
        if self.steps:
            kind = self.kind_of(q)
            for z_last in (True, False):
                @pl.when(kind < 2 if z_last else kind >= 2)
                def _():
                    if e > 0:
                        self.end_step(q, kind, e - 1, z_last)
                    if e < STEPS:
                        self.begin_step(q, kind, e, z_last)

        if e == self.steps:
            self.store(q).start()

    def tick(self, t, done):
        def counts(table):
            def among(ticks, low, high):
                if low == high:
                    return jnp.int32(low)
                middle = (low + high) // 2
                return jnp.where(t >= ticks[middle], among(ticks, middle + 1, high), among(ticks, low, middle))

            return [among([chunk[e] for chunk in table], 0, len(table)) for e in range(self.steps + 1)]

        upto = lax.cond(self.core == 0, lambda: counts(self.table[0]), lambda: counts(self.table[1]))
        for e in reversed(range(self.steps + 1)):
            def one(q, carry):
                self.event(q, e)
                return carry

            lax.fori_loop(done[e], upto[e], one, 0)
        return upto

    def end(self):
        def stored(q, carry):
            self.store(q).wait()
            return carry

        lax.fori_loop(0, ROWS // CHUNK, stored, 0)

        for number in range(len(EMITS) - RING, len(EMITS)):
            for unit, source in self.ring_units(number):
                self.to_partner(unit, source).wait_send()


def backward_kernel(dp, grad_own, own1, halo1, send0, place_back, small, select, back, merge_sums, *refs):
    saved = (refs[0:7], refs[7:14])
    own, other, normed_hbm, cots_hbm = refs[14:18], refs[18:22], refs[22], refs[23]
    total, grad_x = refs[24:26]
    bufs, weights, refs = refs[26:33], refs[33:37], refs[37:]
    gm, n_ref, g_ref, work, score_sum, grad_small, halo_out, halo_in, rows_out, rows_in, page_rows, normed, cots = refs[0:13]
    acc, paired, slots, load_sem, misc_sem = refs[13:18]
    qkv, attn, attended, hidden, act, dgelu, x_ref = bufs
    wqkv, wproj, wfc1, wfc2 = weights
    gpre, dqkv = dgelu, qkv
    ex = Exchange(dp, acc, paired, slots, total, refs[18:23])
    core = ex.core
    tokens = g_ref.shape[0]
    low_masks, masks = head_masks(BF), head_masks(F32)
    def fetch(layer, names):
        for name in names:
            if name < 7:
                pltpu.make_async_copy(saved[layer][name], bufs[name], load_sem.at[layer, name]).start()
            else:
                i = name - 7

                @pl.when(core == layer)
                def _():
                    pltpu.make_async_copy(own[i], weights[i], load_sem.at[layer, name]).start()

                @pl.when(core != layer)
                def _():
                    pltpu.make_async_copy(other[i], weights[i], load_sem.at[layer, name]).start()

    def fetched(layer, *names):
        for name in names:
            target = bufs[name] if name < 7 else weights[name - 7]
            source = saved[0][name] if name < 7 else own[name - 7]
            pltpu.make_async_copy(source, target, load_sem.at[layer, name]).wait()

    def refill(step, names):
        @pl.when(step == 0)
        def _():
            fetch(0, names)

    fetch_order = [10, 5, 4, 3, 9, 2, 8, 0, 1, 7, 6]
    grad_copy = pltpu.make_async_copy(grad_own, g_ref, misc_sem.at[0])
    merge_copies = [pltpu.make_async_copy(normed_hbm, normed, misc_sem.at[6]), pltpu.make_async_copy(cots_hbm, cots, misc_sem.at[7])]
    for copy in merge_copies:
        copy.start()
    grad_copy.start()
    fetch(1, fetch_order)
    ex.greet()
    halo_copy = pltpu.make_async_remote_copy(
        src_ref=halo_out, dst_ref=halo_in, send_sem=misc_sem.at[1], recv_sem=misc_sem.at[2],
        device_id=(ex.partner, ex.me), device_id_type=MESH)
    rows_copy = pltpu.make_async_remote_copy(
        src_ref=rows_out, dst_ref=rows_in, send_sem=misc_sem.at[3], recv_sem=misc_sem.at[4],
        device_id=(ex.partner, ex.me), device_id_type=MESH)
    last_copy = pltpu.make_async_copy(page_rows, grad_x, misc_sem.at[5])
    pages = tokens // (2 * WP)

    def half_of(half):
        return pl.ds(pl.multiple_of(half * 256, 256), 256)

    def send_rows():
        rows_out[...] = g_ref[:, half_of(ex.partner)].astype(BF)
        rows_copy.start()

    def place_rows():
        rows_copy.wait()
        mine = g_ref[:, half_of(core)]
        high = mine.astype(BF)
        low = (mine - high.astype(F32)).astype(BF)
        for p in range(pages):
            rows = slice(p * 2 * WP, (p + 1) * 2 * WP)
            placed = (
                mm(place_back[core], high[rows]) + mm(place_back[core], low[rows]) + mm(place_back[ex.partner], rows_in[rows, :]))
            for r in range(PAGE):
                page_rows[p, r] = placed[r * PAGE : r * PAGE + PAGE]
        last_copy.start()


    def put(row, value):
        grad_small[row : row + 1] = jnp.sum(value, axis=0, keepdims=True)

    def fc2_piece(step, layer, half):
        vectors = small.at[layer]
        owner = core == layer
        if half == 0:
            grad_small[...] = jnp.zeros_like(grad_small)

            @pl.when(step == 0)
            def _():
                grad_copy.wait()

            @pl.when(step == 1)
            def _():
                halo_copy.wait()
                g_ref[...] = g_ref[...] + by_page_back(pages, send0, halo_in[...])

            gm[...] = g_ref[...].astype(BF)
            put(7, gm[...].astype(F32))
            fetched(layer, 10, 5)
        for j in range(half * 4, half * 4 + 4):
            cols = slice(j * 256, j * 256 + 256)
            low = (mm_nt(gm[...], wfc2[cols, :]) * dgelu[:, cols].astype(F32)).astype(BF)
            gpre[:, cols] = low
            grad_small[8 + j // 2 : 9 + j // 2, (j % 2) * 256 : (j % 2) * 256 + 256] = jnp.sum(
                low.astype(F32), axis=0, keepdims=True)
        if half == 0:
            fetched(layer, 4)
        for b in range(half * 2, half * 2 + 2):
            ex.emit(4 + b, owner, mm_tn(act[:, b * 512 : b * 512 + 512], gm[...]).astype(BF))
        if half == 1:
            refill(step, [4, 10])

    def fc1_piece(step, layer):
        fetched(layer, 3)
        unit, _ = unit_norm(hidden[...])
        n_ref[...] = (unit * small[layer, 5:6] + small[layer, 6:7]).astype(BF)
        for b in range(4):
            ex.emit(8 + b, core == layer, mm_tn(n_ref[...], gpre[:, b * 512 : b * 512 + 512]).astype(BF))

    def norm_two_piece(step, layer):
        fetched(layer, 9)
        for j in range(2):
            work[:, j * 256 : j * 256 + 256] = mm_nt(gpre[...], wfc1[j * 256 : j * 256 + 256, :])
        unit, inv_std = unit_norm(hidden[...])
        dn = work[...]
        put(5, dn * unit)
        put(6, dn)
        g_ref[...] = g_ref[...] + unit_norm_back(dn, unit, inv_std, small[layer, 5:6])
        gm[...] = g_ref[...].astype(BF)
        put(4, gm[...].astype(F32))
        refill(step, [5, 3, 9])

    def proj_piece(step, layer):
        fetched(layer, 2, 8)
        ex.emit(12, core == layer, mm_tn(attended[...], gm[...]).astype(BF))
        for j in range(2):
            n_ref[:, j * 256 : j * 256 + 256] = mm_nt(gm[...], wproj[j * 256 : j * 256 + 256, :]).astype(BF)
        score_sum[...] = jnp.zeros_like(score_sum)
        fetched(layer, 0, 1)
        refill(step, [2, 8])

    def window(w, carry):
        rows = aligned(w * WP, WP)
        for blk in range(4):
            cols = [slice(i * 512 + blk * 128, i * 512 + blk * 128 + 128) for i in range(3)]
            q, k, v = [qkv[rows, c] for c in cols]
            g = n_ref[rows, cols[0]]
            a = attn[aligned((w * 4 + blk) * 4 * WP, 4 * WP), :]
            p = mm_nt(stack_heads(g, low_masks), v)
            wide = a.astype(F32)
            ap = wide * p
            low = (ap - wide * jnp.sum(ap, axis=-1, keepdims=True)).astype(BF)
            score_sum[blk * 4 * WP : (blk + 1) * 4 * WP, :] += low.astype(F32)
            gt, qt = g.T, q.T
            dv = [mm(gt[h * 32 : h * 32 + 32], a[h * WP : (h + 1) * WP]) for h in range(4)]
            dk = [mm(qt[h * 32 : h * 32 + 32], low[h * WP : (h + 1) * WP]) * 32**-0.5 for h in range(4)]
            dqkv[rows, cols[2]] = jnp.concatenate(dv, axis=0).astype(BF).T
            dqkv[rows, cols[1]] = jnp.concatenate(dk, axis=0).astype(BF).T
            dqkv[rows, cols[0]] = (pick_heads(mm(low, k), masks) * 32**-0.5).astype(BF)
        return carry

    def attention_piece(step, layer, half):
        count = tokens // WP // 2
        lax.fori_loop(0, count, lambda i, carry: window(half * count + i, carry), 0, unroll=3)

        @pl.when(half == 1)
        def _():
            refill(step, [1])

    def qkv_piece(step, layer):
        fetched(layer, 6)
        unit, _ = unit_norm(x_ref[...].astype(F32))
        n_ref[...] = (unit * small[layer, 0:1] + small[layer, 1:2]).astype(BF)
        for b in range(3):
            ex.emit(13 + b, core == layer, mm_tn(n_ref[...], dqkv[:, b * 512 : b * 512 + 512]).astype(BF))
        put(2, dqkv[:, 0:512].astype(F32))
        put(3, dqkv[:, 1024:1536].astype(F32))

    def norm_one_piece(step, layer):
        fetched(layer, 7)
        for j in range(2):
            work[:, j * 256 : j * 256 + 256] = mm_nt(dqkv[...], wqkv[j * 256 : j * 256 + 256, :])
        unit, inv_std = unit_norm(x_ref[...].astype(F32))
        dn = work[...]
        put(0, dn * unit)
        put(1, dn)
        g_ref[...] = g_ref[...] + unit_norm_back(dn, unit, inv_std, small[layer, 0:1])

        @pl.when(step == 0)
        def _():
            gm[...] = g_ref[...].astype(BF)
            halo_out[...] = by_page_back(pages, halo1, gm[...]).astype(BF)
            halo_copy.start()
            g_ref[...] = by_page_back(pages, own1, gm[...])

        refill(step, [0, 7, 6])
        reduce_table(score_sum, select, back, grad_small.at[16:32])
        grad_small[32:40] = merge_sums[...]
        ex.emit(16, core == layer, jnp.concatenate([grad_small[...], jnp.zeros((UNIT - 48, 512), F32)], axis=0).astype(BF))

    pieces = [partial(fc2_piece, half=0), partial(fc2_piece, half=1), fc1_piece, norm_two_piece, proj_piece,
              attention_piece, None, qkv_piece, norm_one_piece]

    for copy in merge_copies:
        copy.wait()
    for half in range(2):
        for k in range(4):
            ex.emit(k, core == half, mm_tn(normed[:, k * 512 : k * 512 + 512], cots[half]).astype(BF))

    def tick(t, done):
        done = ex.tick(t, done)
        step, place = t // len(pieces), lax.rem(t, len(pieces))
        layer = 1 - step
        for i, piece in enumerate(pieces):
            if piece is attention_piece:
                @pl.when(jnp.logical_and(jnp.logical_or(place == i, place == i + 1), step < 2))
                def _():
                    attention_piece(step, layer, place - i)
            elif piece is not None:
                @pl.when(jnp.logical_and(place == i, step < 2))
                def _():
                    piece(step, layer)

        @pl.when(t == 2 * len(pieces))
        def _():
            send_rows()

        @pl.when(t == 2 * len(pieces) + 2)
        def _():
            place_rows()

        return done

    ticks = 1 + max(t for core in ex.table for chunk in core for t in chunk)
    lax.fori_loop(0, max(ticks, 2 * len(pieces) + 3), tick, [jnp.int32(0)] * (ex.steps + 1))
    ex.end()
    last_copy.wait()


def widen_kernel(total, page_rows, merged_rows, turn, wqkv, wproj, wfc1, wfc2, wmerge, pages_out, *refs):
    singles, (fc1_bias, merge_gain, merge_bias, table, merged, rows, stage, passing, wide, load_sem, store_sem, pass_sem) = refs[0:8], refs[8:]
    pass_in = pltpu.make_async_copy(page_rows, passing, pass_sem.at[0])
    pass_out = pltpu.make_async_copy(passing, pages_out, pass_sem.at[1])
    pass_in.start()
    blocks = [(b * 512, wmerge.at[b * 512 : b * 512 + 512, :]) for b in range(4)]
    blocks += [(2048 + b * 512, wfc2.at[b * 512 : b * 512 + 512, :]) for b in range(4)]
    blocks += [(4096 + b * 512, wfc1.at[:, b * 512 : b * 512 + 512]) for b in range(4)]
    blocks += [(6144, wproj)]
    blocks += [(6656 + b * 512, wqkv.at[:, b * 512 : b * 512 + 512]) for b in range(3)]
    loads = []
    for i, (start, _) in enumerate(blocks + [(8192, None)]):
        count = min(512, total.shape[0] - start)
        copy = pltpu.make_async_copy(total.at[start : start + count], rows.at[start : start + count], load_sem.at[i])
        copy.start()
        loads.append(copy)
    stores = []
    for i, (start, target) in enumerate(blocks):
        slot = i % 4
        loads[i].wait()
        if i == 1:
            pass_in.wait()
            pass_out.start()
        if i >= 4:
            stores[i - 4].wait()
        stage[slot] = rows[start : start + 512, :].astype(F32)
        copy = pltpu.make_async_copy(stage.at[slot], target, store_sem.at[slot])
        copy.start()
        stores.append(copy)
    wide[...] = merged_rows[...].astype(F32)
    group = wide.shape[0] // AREA
    for place in range(AREA):
        merged[place // 10, place % 10] = wide[place * group : place * group + merged.shape[2], :].astype(BF)
    loads[-1].wait()
    tail = rows[8192:8240, :].astype(F32)
    for k in range(8):
        singles[k][...] = tail[k : k + 1]
    for k in range(4):
        cols = slice(k * 512, k * 512 + 512)
        fc1_bias[:, cols] = tail[8 + k : 9 + k]
        merge_gain[:, cols] = tail[32 + k : 33 + k]
        merge_bias[:, cols] = tail[36 + k : 37 + k]
    high = rows[8208:8224, 0:384].astype(BF)
    table[...] = mm(high, turn[...])
    for copy in stores[-4:]:
        copy.wait()
    pass_out.wait()


HBM = pl.BlockSpec(memory_space=pl.ANY)
VMEM = pl.BlockSpec(memory_space=pltpu.VMEM)


def scratch_of(entry):
    if entry is None:
        return pltpu.SemaphoreType.DMA
    if isinstance(entry, int):
        return pltpu.SemaphoreType.DMA((entry,))
    if isinstance(entry[0], int):
        return pltpu.SemaphoreType.DMA(entry)
    return pltpu.VMEM(*entry)


def call(kernel, args, outs, scratch, name, collective_id=None):
    return pl.pallas_call(
        kernel,
        out_shape=[jax.ShapeDtypeStruct(s, d) for s, d, _ in outs],
        in_specs=[spec for _, spec in args],
        out_specs=[spec for _, _, spec in outs],
        scratch_shapes=[scratch_of(s) for s in scratch],
        compiler_params=pltpu.CompilerParams(
            vmem_limit_bytes=VMEM_LIMIT, collective_id=collective_id, has_side_effects=collective_id is not None),
        name=name,
    )(*[value for value, _ in args])


def shards(
    page_inputs, gain_one, bias_one, qkv_weight, query_bias, value_bias, bias_table, proj_weight, proj_bias,
    gain_two, bias_two, fc1_weight, fc1_bias, fc2_weight, fc2_bias, merge_gain, merge_bias, merge_weight, cotangent,
):
    dp = lax.axis_size("dp")
    pages = page_inputs.shape[0]
    tokens = pages * 2 * WP
    heads = bias_table.shape[2]
    table = bias_table.shape[1]
    place = place_tables(pages)
    select, back = code_matrices()
    merged_rows, cot_rows = place["pick"].shape[1:]

    turned = np.zeros((table, 384), np.float32)
    for u in range(table):
        turned[table - 1 - u, (u - 4) % 384] = 1
    params = [gain_one, bias_one, query_bias, value_bias, proj_bias, gain_two, bias_two, fc2_bias, fc1_bias,
              merge_gain.reshape(16, 128), merge_bias.reshape(16, 128), bias_table[0].T, jnp.asarray(turned, BF)]
    own = [qkv_weight[0], proj_weight[0], fc1_weight[0], fc2_weight[0]]

    def at(spec, *values):
        return [(v, spec) for v in values]

    rows = ((tokens, 512), BF)
    wide_rows = ((tokens, 512), F32)
    saved_shapes = [((tokens, 1536), BF), ((pages * 2 * heads * WP, WP), BF), rows, wide_rows,
                    ((tokens, 2048), BF), ((tokens, 2048), BF)]
    weight_shapes = [(w.shape, BF) for w in own]
    halo = ((pages * WP, 512), BF)
    halos = ((3, pages * WP, 512), BF)
    parts_shape = ((2, 2048, 512), BF)
    mrows = (merged_rows, 512)
    results = call(
        forward_kernel,
        at(VMEM, page_inputs, cotangent.transpose(1, 2, 0, 3), *params, window_masks(),
                                    *[place[n] for n in ("take", "pick", "send0", "own1", "halo1", "own2", "halo2")], select)
        + at(HBM, place["own2_back"], place["halo2_back"]) + at(HBM, *own, merge_weight),
        [(*shape, HBM) for shape in (saved_shapes + [rows]) * 2 + weight_shapes]
        + [((cot_rows, 512), BF, VMEM), ((merged_rows, 2048), BF, HBM), ((2, *mrows), BF, HBM), ((8, 512), F32, VMEM), ((2, 16, 512), F32, VMEM), (*wide_rows, VMEM)],
        weight_shapes * 2 + [parts_shape] + saved_shapes
        + [rows, rows, ((heads * WP, WP), BF), ((2, pages * 400, 256), BF), ((2, 32, 512), BF), ((2, cot_rows, 512), BF), rows, halos, halos,
           ((merged_rows, 2048), F32), ((merged_rows, 2048), F32), ((2, *mrows), BF), (mrows, BF), ((cot_rows, 512), F32), ((pages * 400, 256), F32),
           ((merged_rows, 2048), BF), ((2, *mrows), BF), ((tokens, 4 * merged_rows), BF), ((pages * WP, 4 * merged_rows), BF),
           8, (2, 7), 4, 12, 12, 4],
        "forward", collective_id=1)
    saved0, saved1, other = results[0:7], results[7:14], results[14:18]
    merged, normed, cots, merge_sums, small, grad_own = results[18:]

    chunks, units = ROWS // CHUNK, ROWS // UNIT
    page_half = ((pages, PAGE, PAGE, 256), F32)
    total, grad_pages = call(
        partial(backward_kernel, dp),
        at(HBM, grad_own) + at(VMEM, place["own1"], place["halo1"], place["send0"], place["back"], small, select, back, merge_sums)
        + at(HBM, *saved0, *saved1, *own, *other, normed, cots),
        [((ROWS, 512), BF, HBM), (*page_half, HBM)],
        saved_shapes + [rows] + weight_shapes
        + [rows, rows, wide_rows, wide_rows, ((heads * WP, WP), F32), ((48, 512), F32), halo, halo,
           ((tokens, 256), BF), ((tokens, 256), BF), page_half, ((merged_rows, 2048), BF), ((2, *mrows), BF)]
        + [((ROWS + RING * 512, 512), BF), ((ROWS, 512), BF), ((chunks * SLOT, 512), BF), (2, 11), 8,
           units, units, chunks, (chunks, STEPS), (chunks, STEPS)],
        "backward", collective_id=0)
    if dp != CHIPS:
        total = lax.psum(total.astype(F32), "dp")

    turn = np.zeros((384, table), np.float32)
    for u in range(table):
        turn[u + 3, table - 1 - u] = 1
    wide_row = ((1, 2048), F32, VMEM)
    g_qkv, g_proj, g_fc1, g_fc2, g_merge, grad_pages, *single, g_fc1_bias, g_gain, g_bias, g_table, merged = call(
        widen_kernel, at(HBM, total, grad_pages) + at(VMEM, merged, jnp.asarray(turn, BF)),
        [((512, 1536), F32, HBM), ((512, 512), F32, HBM), ((512, 2048), F32, HBM), ((2048, 512), F32, HBM),
         ((2048, 512), F32, HBM), (*page_half, HBM)] + [((1, 512), F32, VMEM)] * 8
        + [wide_row, wide_row, wide_row, ((heads, table), F32, VMEM), ((10, 10, pages, 512), BF, VMEM)],
        [((ROWS, 512), total.dtype), ((4, 512, 512), F32), page_half, ((cot_rows, 512), F32), 17, 4, 2], "widen")
    return (
        merged.transpose(2, 0, 1, 3), grad_pages,
        single[0], single[1], g_qkv[None], single[2], single[3], g_table.T[None], g_proj[None], single[4], single[5], single[6],
        g_fc1[None], g_fc1_bias, g_fc2[None], single[7], g_gain.reshape(2048), g_bias.reshape(2048), g_merge,
    )


def solution(mesh):
    row, mat = P("pipe", None), P("pipe", None, None)
    wide = P("dp", None, None, "pipe")
    in_specs = (wide, row, row, mat, row, row, mat, mat, row, row, row, mat, row, mat, row, P(), P(), P(None, "pipe"), wide)
    out_specs = (wide, wide, row, row, mat, row, row, mat, mat, row, row, row, mat, row, mat, row, P(), P(), P(None, "pipe"))
    return jax.shard_map(shards, mesh=mesh, in_specs=in_specs, out_specs=out_specs, check_vma=False)
```
